32 devices in a mesh: dp: 8 (over z, y), head: 4 (over x, core).
Axes of the slice: x: 2, y: 2, z: 4, core: 2. Of those that a mesh axis runs over, the one named last changes fastest.
Arguments:
- queries: bfloat16 [2048, 1536], P(('dp', 'head')), may hold values from -100 to 100
- fresh_keyvals: bfloat16 [2048, 512], P(('dp', 'head')), may hold values from -4.1 to 4.1
- ssm_input: bfloat16 [2048, 3072], P(('dp', 'head')), may hold values from -4 to 4
- gate_input: bfloat16 [2048, 3072], P(('dp', 'head')), may hold values from -40 to 40
- state_maps: bfloat16 [2048, 512], P(('dp', 'head')), may hold values from -4 to 4
- step_logit: bfloat16 [2048, 24], P(('dp', 'head')), may hold values from -6 to 8
- slot_mask: int32 [2048], P(('dp', 'head')), may hold values 0 or 1
- cache_pool: bfloat16 [64, 32, 256], P('dp', 'head'), may hold values from -4 to 4
- page_map: int32 [8, 8], P('dp'), may hold values from 0 to 7, each once within a row
- cached_lengths: int32 [8], P('dp'), may hold values from 1 to 128, 512 in all
- prior_state: bfloat16 [8, 24, 128, 256], P('dp', 'head'), may hold values from -0.8984375 to 0.8984375
- decay_log: float32 [24], P('head'), may hold values from -4.61 to 0.7
- step_bias: float32 [24], P('head'), may hold values from -1 to 1
- skip_gain: float32 [24], P('head'), may hold values from 0.5 to 1.5
- norm_gain: float32 [3072], replicated, may hold values from 0.1 to 1.9
Outputs:
- mixed: bfloat16 [2048, 4608], P(('dp', 'head'))
The draws below stay inside these ranges and needn't reach their ends.
Inputs may be any that keep to these rules, and one draw needn't show every extreme that they name: `page_map`: each row is a permutation of 0 to 7. `cached_lengths`: the lengths sum to 512; the largest is exactly 128.
All inputs are finite; a program needn't handle non-finite values. No bound on the sum of `slot_mask` or of `cached_lengths` on one device may be relied on, other than what follows from the above.
Results may differ from the reference program's by a relative error of at most 0.012.
Values may be sent and summed in bfloat16 or wider, within the bound.
No kernel may reach another device: no remote copies, remote signals or barrier semaphores. Data moves between devices by JAX's collectives and lax.ppermute only.
A program may use at most 64 MiB of HBM per device.

```python
import math
import jax
import jax.numpy as jnp
import numpy as np
from jax import lax

HD = 128
QH = 12
KVH = 2
MAMBA_HEADS = 24
MD = 128
STATE = 256
SPAN = 256
MI = 3072
REQUESTS = 8
TOKEN_SLOTS = 2048
MAXLEN = 128
HALF = 8
N_DP = 8


def attention_streams(key):
    base_keys = jnp.clip(jax.random.normal(jax.random.fold_in(key, 11), (TOKEN_SLOTS, KVH, HD), jnp.float32), -4.0, 4.0)
    base_values = jnp.clip(jax.random.normal(jax.random.fold_in(key, 12), (TOKEN_SLOTS, KVH, HD), jnp.float32), -4.0, 4.0)
    base_queries = 2.5 * jnp.clip(jax.random.normal(jax.random.fold_in(key, 13), (TOKEN_SLOTS, QH, HD), jnp.float32), -4.0, 4.0)
    return (base_queries, base_keys, base_values)


def draw_queries(key, part):
    base_queries, base_keys, base_values = attention_streams(key)
    return base_queries.reshape(TOKEN_SLOTS, QH * HD).astype(jnp.bfloat16)


def draw_fresh_keyvals(key, part):
    base_queries, base_keys, base_values = attention_streams(key)
    stacked = jnp.stack([base_keys, base_values], axis=2)
    return stacked.reshape(TOKEN_SLOTS, 2 * KVH * HD).astype(jnp.bfloat16)


def draw_gate_input(key, part):
    noise = jnp.clip(jax.random.normal(jax.random.fold_in(key, 21), (TOKEN_SLOTS, MI), jnp.float32), -4.0, 4.0)
    row_scale = jnp.exp(jax.random.uniform(jax.random.fold_in(key, 22), (TOKEN_SLOTS, 1), jnp.float32, 0.0, 1.15))
    column_scale = jnp.exp(jax.random.uniform(jax.random.fold_in(key, 23), (1, MI), jnp.float32, 0.0, 1.15))
    return (noise * row_scale * column_scale).astype(jnp.bfloat16)


def draw_step_logit(key, part):
    start_offset = jnp.clip(jax.random.normal(jax.random.fold_in(key, 31), (TOKEN_SLOTS, MAMBA_HEADS), jnp.float32), -4.0, 4.0) * 0.5 - 4.0
    request_spans = jax.random.randint(jax.random.fold_in(key, 32), (TOKEN_SLOTS, MAMBA_HEADS), 0, 200) == 0
    return jnp.where(request_spans, start_offset + 10.0, start_offset).astype(jnp.bfloat16)


def draw_decay_log(key, part):
    values = jax.random.uniform(jax.random.fold_in(key, 41), (MAMBA_HEADS,), jnp.float32, -3.5, 0.69)
    return values


def with_ends(array, key, least, top_value):
    index_at = [jax.random.randint(jax.random.fold_in(key, axis), (), 0, length) for axis, length in enumerate(array.shape)]
    main_axis = array.shape.index(max(array.shape))
    beside = index_at[:main_axis] + [(index_at[main_axis] + 1) % array.shape[main_axis]] + index_at[main_axis + 1:]
    return array.at[tuple(index_at)].set(least).at[tuple(beside)].set(top_value)


def levels(rng, dims, cuts, low, high):
    loudness, own = 1.0, jax.random.fold_in(rng, 6)
    for axis_at, shards_of in cuts:
        steps = jnp.exp(jax.random.uniform(jax.random.fold_in(own, axis_at), (shards_of,), jnp.float32, low / len(cuts), high / len(cuts)))
        loudness = loudness * jnp.repeat(steps, dims[axis_at] // shards_of).reshape([-1 if axis == axis_at else 1 for axis in range(len(dims))])
    return loudness


def length_profile(number_of, total, limit, lean):
    portions = [(1 << 20) // math.isqrt(rank ** lean) + 1 for rank in range(2, number_of + 1)]
    spare, holding = total - limit - (number_of - 1), [1] * (number_of - 1)
    while spare > 0:
        candidates = [i for i in range(number_of - 1) if holding[i] < limit]
        mass, budget = sum([portions[i] for i in candidates]), spare
        for i in candidates:
            extra = min(limit - holding[i], max(1, budget * portions[i] // mass), spare)
            holding[i] = holding[i] + extra
            spare = spare - extra
    return np.array([limit] + holding)


def ragged_sizes(rng, count, total, limit, lean):
    if count == 2:
        one = jax.random.randint(rng, (), max(1, total - limit), min(limit, total - 1) + 1)
        return jnp.stack([one, total - one])
    tallies = jnp.asarray(length_profile(count, total, limit, lean), jnp.int32)
    couples = (count - 1) // 2
    source_of, sink = tallies[1:1 + 2 * couples:2], tallies[2:2 + 2 * couples:2]
    margin = jnp.minimum(source_of - 1, limit - sink)
    shifted = jax.random.randint(jax.random.fold_in(rng, 1), (couples,), 0, 1 << 20) % (margin + 1)
    tallies = tallies.at[1:1 + 2 * couples:2].set(source_of - shifted).at[2:2 + 2 * couples:2].set(sink + shifted)
    return tallies[jax.random.permutation(jax.random.fold_in(rng, 2), count)]


def centred(rng, extent, deviation, bound, shards=(), kind=jnp.bfloat16):
    array = deviation * jax.random.normal(rng, extent, jnp.float32)
    if shards:
        array = array * levels(rng, extent, shards, -0.22, 0.18)
    return jnp.clip(array, -bound, bound).astype(kind)


def setup_inputs(seed: int = 0) -> dict:
    key_of = jax.random.split(jax.random.key(seed), 16)
    queries = draw_queries(jax.random.fold_in(key_of[15], 71), 0)
    fresh_keyvals = draw_fresh_keyvals(jax.random.fold_in(key_of[15], 71), 0)
    ssm_input = centred(key_of[2], (TOKEN_SLOTS, MI), 1.0, 4.0, ((0, 32),))
    gate_input = draw_gate_input(jax.random.fold_in(key_of[15], 71), 0)
    state_maps = centred(key_of[4], (TOKEN_SLOTS, 2 * STATE), 1.0, 4.0, ((0, 32),))
    step_logit = draw_step_logit(jax.random.fold_in(key_of[15], 71), 0)
    slot_mask = with_ends((jax.random.randint(key_of[6], (TOKEN_SLOTS,), 0, 8) < 7).astype(jnp.int32), jax.random.fold_in(key_of[6], 1), 0, 1)
    cache_pool = centred(key_of[7], (N_DP * REQUESTS, 2 * KVH * HALF, 2 * HD), 1.0, 4.0, ((0, 8), (1, 4)))
    page_map = jax.vmap(lambda own: jax.random.permutation(own, N_DP))(jax.random.split(key_of[8], REQUESTS)).reshape((REQUESTS, N_DP)).astype(jnp.int32)
    cached_lengths = ragged_sizes(key_of[9], REQUESTS, REQUESTS * MAXLEN // 2, MAXLEN, 1).astype(jnp.int32)
    prior_state = centred(key_of[10], (REQUESTS, MAMBA_HEADS, MD, STATE), 0.15, 0.8984375, ((0, 8), (1, 4)))
    decay_log = draw_decay_log(jax.random.fold_in(key_of[15], 71), 0)
    step_bias = jnp.clip(jax.random.uniform(key_of[12], (MAMBA_HEADS,), jnp.float32, -1.0, 1.0) * levels(key_of[12], (MAMBA_HEADS,), ((0, 4),), -0.4, 0.0), -1.0, 1.0)
    skip_gain = jnp.clip(0.5 + 1.0 * jax.random.uniform(key_of[13], (MAMBA_HEADS,), jnp.float32) ** levels(key_of[13], (MAMBA_HEADS,), ((0, 4),), -0.2, 0.2), 0.5, 1.5)
    norm_gain = jnp.clip(1.0 + 0.18 * jax.random.normal(key_of[14], (MI,), jnp.float32), 0.1, 1.9)
    return dict(queries=queries, fresh_keyvals=fresh_keyvals, ssm_input=ssm_input, gate_input=gate_input, state_maps=state_maps, step_logit=step_logit, slot_mask=slot_mask, cache_pool=cache_pool, page_map=page_map, cached_lengths=cached_lengths, prior_state=prior_state, decay_log=decay_log, step_bias=step_bias, skip_gain=skip_gain, norm_gain=norm_gain)


HIGHEST = lax.Precision.HIGHEST
EPSILON = 1e-05

def attention(query_rows, all_keys, all_values, cached_count, valid_rows):
    length = query_rows.shape[0]
    key_count = all_keys.shape[0]
    cached_positions = key_count - length
    row_block = min(512, length)
    inv_scale = 1.0 / math.sqrt(HD)
    key_slots = jnp.arange(key_count, dtype=jnp.int32)
    new_index = key_slots - cached_positions
    live_new = jnp.concatenate([jnp.zeros((cached_positions,), dtype=bool), valid_rows])
    key_live = jnp.where(key_slots < cached_positions, key_slots < cached_count, live_new)
    results = []
    for head_num in range(query_rows.shape[1] // HD):
        pieces = []
        for offset in range(0, length, row_block):
            block_query = query_rows[offset:offset + row_block, head_num * HD:(head_num + 1) * HD]
            row_ids = offset + jnp.arange(row_block, dtype=jnp.int32)
            allowed = key_live[None, :] & ((key_slots[None, :] < cached_positions) | (new_index[None, :] <= row_ids[:, None]))
            scores = jnp.dot(block_query, all_keys.T, preferred_element_type=jnp.float32) * inv_scale
            scores = jnp.where(allowed, scores, -jnp.inf)
            row_max = lax.optimization_barrier(jnp.max(scores, axis=1, keepdims=True))
            exp_terms = jnp.exp(scores - row_max)
            row_total = lax.optimization_barrier(jnp.sum(exp_terms, axis=1, keepdims=True))
            weighted_values = jnp.dot(exp_terms.astype(jnp.bfloat16), all_values, preferred_element_type=jnp.float32)
            pieces.append(weighted_values / row_total)
        results.append(jnp.concatenate(pieces, axis=0))
    joined = jnp.concatenate(results, axis=1) * valid_rows[:, None].astype(jnp.float32)
    return joined.astype(jnp.bfloat16)

def block_scan(inputs, in_raw, out_raw, steps, log_decay, carried):
    length = inputs.shape[0]
    block_len = min(128, length)
    causal = jnp.arange(block_len)[:, None] >= jnp.arange(block_len)[None, :]
    outputs = []
    for offset in range(0, length, block_len):
        block_input = inputs[offset:offset + block_len]
        block_in_raw = in_raw[offset:offset + block_len]
        block_out_raw = out_raw[offset:offset + block_len]
        block_in_map = block_in_raw.astype(jnp.float32)
        block_out_map = block_out_raw.astype(jnp.float32)
        block_steps = steps[offset:offset + block_len]
        cumulative = jnp.cumsum(log_decay[offset:offset + block_len], axis=0)
        log_gaps = cumulative[:, None, :] - cumulative[None, :, :]
        decays = jnp.exp(jnp.where(causal[:, :, None], log_gaps, -jnp.inf))
        intersections = jnp.dot(block_out_raw, block_in_raw.T, preferred_element_type=jnp.float32)
        weights = intersections[:, :, None] * decays * block_steps[None, :, :]
        within = jnp.einsum('tsh,shp->thp', weights, block_input, precision=HIGHEST)
        from_state = jnp.einsum('tn,hpn->thp', block_out_map, carried, precision=HIGHEST) * jnp.exp(cumulative)[:, :, None]
        outputs.append(within + from_state)
        tail_weight = jnp.exp(cumulative[-1:, :] - cumulative) * block_steps
        carried = carried * jnp.exp(cumulative[-1])[:, None, None] + jnp.einsum('shp,sn->hpn', block_input * tail_weight[:, :, None], block_in_map, precision=HIGHEST)
    return jnp.concatenate(outputs, axis=0)

def state_space(inputs, maps, step_rows, valid_rows, decay_log, step_bias, skip_gain, prior):
    length = inputs.shape[0]
    head_count = decay_log.shape[0]
    valid_float = valid_rows.astype(jnp.float32)
    steps = jax.nn.softplus(step_rows.astype(jnp.float32) + step_bias[None, :]) * valid_float[:, None]
    log_decay = -jnp.exp(decay_log)[None, :] * steps
    input_float = inputs.astype(jnp.float32).reshape(length, head_count, -1)
    in_raw = maps[:, :STATE]
    out_raw = maps[:, STATE:]
    result = block_scan(input_float, in_raw, out_raw, steps, log_decay, prior.astype(jnp.float32))
    result = (result + skip_gain[None, :, None] * input_float) * valid_float[:, None, None]
    return result.reshape(length, -1).astype(jnp.bfloat16)

def reference(queries, fresh_keyvals, ssm_input, gate_input, state_maps, step_logit, slot_mask, cache_pool, page_map, cached_lengths, prior_state, decay_log, step_bias, skip_gain, norm_gain):
    pool = cache_pool.reshape(REQUESTS, REQUESTS, KVH, 2, HALF, 2 * HD)
    group_size = QH // KVH

    def one_request(request):
        first_row = (request * SPAN).astype(jnp.int32)
        query_rows = lax.dynamic_slice_in_dim(queries, first_row, SPAN, 0)
        keyval_rows = lax.dynamic_slice_in_dim(fresh_keyvals, first_row, SPAN, 0)
        input_rows = lax.dynamic_slice_in_dim(ssm_input, first_row, SPAN, 0)
        gate_rows = lax.dynamic_slice_in_dim(gate_input, first_row, SPAN, 0)
        map_rows = lax.dynamic_slice_in_dim(state_maps, first_row, SPAN, 0)
        step_rows = lax.dynamic_slice_in_dim(step_logit, first_row, SPAN, 0)
        valid_rows = lax.dynamic_slice_in_dim(slot_mask, first_row, SPAN, 0) > 0
        holders = lax.dynamic_index_in_dim(page_map, request, 0, keepdims=False)
        pool_rows = lax.dynamic_index_in_dim(pool, request, 1, keepdims=False)
        page_rows = jnp.take(pool_rows, holders, axis=0)
        cached_count = lax.dynamic_index_in_dim(cached_lengths, request, 0, keepdims=False)
        prior = lax.dynamic_index_in_dim(prior_state, request, 0, keepdims=False)
        attended_parts = []
        for group in range(KVH):
            cache_rows = page_rows[:, group].reshape(MAXLEN, 2 * HD)
            all_keys = jnp.concatenate([cache_rows[:, :HD], keyval_rows[:, 2 * group * HD:(2 * group + 1) * HD]], axis=0)
            all_values = jnp.concatenate([cache_rows[:, HD:], keyval_rows[:, (2 * group + 1) * HD:(2 * group + 2) * HD]], axis=0)
            group_queries = query_rows[:, group * group_size * HD:(group + 1) * group_size * HD]
            attended_parts.append(attention(group_queries, all_keys, all_values, cached_count, valid_rows))
        attended = jnp.concatenate(attended_parts, axis=1)
        scanned = state_space(input_rows, map_rows, step_rows, valid_rows, decay_log, step_bias, skip_gain, prior)
        gated = scanned.astype(jnp.float32) * jax.nn.silu(gate_rows.astype(jnp.float32))
        normed = gated * lax.rsqrt(lax.optimization_barrier(jnp.mean(gated * gated, axis=1, keepdims=True)) + EPSILON) * norm_gain[None, :]
        return jnp.concatenate([attended, normed.astype(jnp.bfloat16)], axis=1)
    stacked = lax.map(one_request, jnp.arange(REQUESTS, dtype=jnp.int32))
    return stacked.reshape(TOKEN_SLOTS, QH * HD + MI)
```

```python
import math

import jax
import jax.numpy as jnp
from jax import lax
from jax.experimental import pallas as pl
from jax.experimental.pallas import tpu as pltpu
from jax.sharding import PartitionSpec as P

HD = 128
QH = 12
KVH = 2
GROUP = QH // KVH
STATE = 256
MI = 3072
PAGE = 16
LANES = 128
EPSILON = 1e-05
BF16 = jnp.bfloat16
F32 = jnp.float32
HIGHEST = lax.Precision.HIGHEST
VMEM = pl.BlockSpec(memory_space=pltpu.VMEM)
SMEM = pl.BlockSpec(memory_space=pltpu.SMEM)


def call(kernel, outs, specs, scratch=(), limit=24 << 20):
    return pl.pallas_call(
        kernel,
        out_shape=[jax.ShapeDtypeStruct(shape, dtype) for shape, dtype in outs],
        in_specs=specs,
        out_specs=[VMEM] * len(outs),
        scratch_shapes=list(scratch),
        compiler_params=pltpu.CompilerParams(vmem_limit_bytes=limit),
    )


def columns(ref, owner, width):
    return ref[:, pl.ds(pl.multiple_of(owner * width, LANES), width)]


def iota(shape, dim):
    return lax.broadcasted_iota(jnp.int32, shape, dim)


def nt_dot(a, b, precision=None):
    return lax.dot_general(
        a, b, (((1,), (1,)), ((), ())), preferred_element_type=F32, precision=precision
    )


def pack_kernel(x_ref, maps_ref, logit_ref, mask_ref, small_ref, x1_ref, x2_ref, x3_ref):
    me = lax.axis_index("head")
    rows = x_ref.shape[0]
    width = x1_ref.shape[1]
    maps_width = maps_ref.shape[1]
    heads = logit_ref.shape[1]
    small_ref[:, :maps_width] = maps_ref[...]
    diagonal = iota((rows, rows), 0) == iota((rows, rows), 1)
    mask_row = jnp.broadcast_to(mask_ref[...], (rows, rows))
    mask_column = jnp.sum(
        jnp.where(diagonal & (mask_row > 0), 1.0, 0.0), axis=1, keepdims=True
    )
    small_ref[:, maps_width:] = jnp.broadcast_to(mask_column, (rows, LANES)).astype(BF16)
    small_ref[:, maps_width : maps_width + heads] = logit_ref[...]
    for hop, ref in ((1, x1_ref), (2, x2_ref), (3, x3_ref)):
        ref[...] = columns(x_ref, me ^ hop, width)


def scan_kernel(
    log_rate_ref, bias_ref, skip_ref,
    small0, small1, small2, small3, x_ref, x1, x2, x3, prior_ref,
    y0, y1, y2, y3,
    small, xs, ys,
):
    me = lax.axis_index("head")
    rows, width = x1.shape
    span = 4 * rows
    head_count = width // HD
    maps_width = 2 * STATE
    every_head = 4 * head_count
    def at(hop):
        return pl.ds(pl.multiple_of((me ^ hop) * rows, rows), rows)
    for hop, ref in enumerate((small0, small1, small2, small3)):
        small[at(hop), :] = ref[...]
    xs[at(0), :] = columns(x_ref, me, width)
    for hop, ref in ((1, x1), (2, x2), (3, x3)):
        xs[at(hop), :] = ref[...]

    logits = small[:, maps_width:]
    first = me * head_count
    pick_row, pick_lane = iota((8, LANES), 0), iota((8, LANES), 1)
    picked = jnp.where(pick_row < head_count, pick_row + first, every_head)
    by_row = jnp.where(picked == pick_lane, 1.0, 0.0).astype(BF16)
    pick_lane, pick_row = iota((LANES, LANES), 0), iota((LANES, LANES), 1)
    picked = jnp.where(pick_row < head_count, pick_row + first, every_head)
    by_lane = jnp.where(picked == pick_lane, 1.0, 0.0).astype(BF16)
    row_logits = nt_dot(by_row, logits)
    lane_logits = jnp.dot(logits, by_lane, preferred_element_type=F32)
    row_mask = row_logits[head_count : head_count + 1, :]
    lane_mask = lane_logits[:, head_count : head_count + 1]

    row_head, lane_head = iota((8, 1), 0), iota((1, LANES), 1)
    row_bias = row_rate = jnp.zeros((8, 1), F32)
    lane_bias = lane_rate = jnp.zeros((1, LANES), F32)
    for head in range(head_count):
        bias, log_rate = bias_ref[head], log_rate_ref[head]
        row_bias = jnp.where(row_head == head, bias, row_bias)
        row_rate = jnp.where(row_head == head, log_rate, row_rate)
        lane_bias = jnp.where(lane_head == head, bias, lane_bias)
        lane_rate = jnp.where(lane_head == head, log_rate, lane_rate)
    row_steps = jnp.log(1.0 + jnp.exp(row_logits + row_bias)) * row_mask
    lane_steps = jnp.log(1.0 + jnp.exp(lane_logits + lane_bias)) * lane_mask
    row_decay = -jnp.exp(row_rate) * row_steps
    lane_decay = -jnp.exp(lane_rate) * lane_steps
    token, source = iota((span, span), 0), iota((span, span), 1)
    upto = jnp.where(source <= token, 1.0, 0.0)
    row_sum = nt_dot(row_decay, upto, HIGHEST)
    lane_sum = jnp.dot(upto, lane_decay, preferred_element_type=F32, precision=HIGHEST)
    row_shift = row_sum - jnp.log(row_steps)

    in_map, out_map = small[:, :STATE], small[:, STATE : 2 * STATE]
    products = nt_dot(out_map, in_map)
    prior = prior_ref[0].reshape(width, STATE)
    from_prior = nt_dot(out_map, prior)
    causal = source <= token
    for head in range(head_count):
        cols = slice(head * HD, (head + 1) * HD)
        total = lane_sum[:, head : head + 1]
        gaps = jnp.where(causal, total - row_shift[head : head + 1, :], -jnp.inf)
        weights = (jnp.exp(gaps) * products).astype(BF16)
        x = xs[:, cols]
        y = jnp.dot(weights, x, preferred_element_type=F32)
        y = y + from_prior[:, cols] * jnp.exp(total) + skip_ref[head] * x.astype(F32)
        ys[:, cols] = (y * lane_mask).astype(BF16)
    for hop, ref in enumerate((y0, y1, y2, y3)):
        ref[...] = ys[at(hop), :]


def attention_kernel(
    page_map_ref, length_ref, query_ref, pages_ref, kv0, kv1, kv2, kv3, small0, small1, small2, small3, out_ref
):
    me = lax.axis_index("head")
    rows = query_ref.shape[0]
    slots = page_map_ref.shape[1]
    cached = slots * PAGE
    inv_scale = 1.0 / math.sqrt(HD)
    maps_width = 2 * STATE
    lane = iota((1, cached), 1)

    def place(page, base):
        return jnp.where(lane // PAGE == page_map_ref[0, page], page * PAGE, base)

    position = lax.fori_loop(0, slots, place, jnp.zeros((1, cached), jnp.int32), unroll=slots <= 8)
    position = position + lane % PAGE
    shut = [jnp.broadcast_to(jnp.where(position < length_ref[0], 0.0, -jnp.inf), (rows, cached))]
    ones = jnp.where(iota((8, LANES), 1) == LANES - 1, 1.0, 0.0).astype(BF16)
    token, source = iota((rows, rows), 0), iota((rows, rows), 1)
    own_mask = None
    for hop, ref in enumerate((small0, small1, small2, small3)):
        real = nt_dot(ones, ref[:, maps_width:])[0:1, :] > 0.5
        limit = token if hop == 0 else jnp.where((me ^ hop) < me, rows, -1)
        shut.append(jnp.where(real & (source <= limit), 0.0, -jnp.inf))
    shut = jnp.concatenate(shut, axis=1)
    shut = jnp.concatenate([shut] * GROUP, axis=0)
    keep = small0[:, maps_width + LANES - 1 :].astype(F32)
    pages = pages_ref[...].reshape(slots, KVH, PAGE, 2 * HD)
    for group in range(KVH):
        queries = jnp.concatenate(
            [query_ref[:, (group * GROUP + h) * HD : (group * GROUP + h + 1) * HD] for h in range(GROUP)],
            axis=0,
        )
        old = pages[:, group].reshape(cached, 2 * HD)
        base = 2 * group * HD
        keys = jnp.concatenate(
            [old[:, :HD]] + [ref[:, base : base + HD] for ref in (kv0, kv1, kv2, kv3)], axis=0
        )
        values = jnp.concatenate(
            [old[:, HD:]] + [ref[:, base + HD : base + 2 * HD] for ref in (kv0, kv1, kv2, kv3)], axis=0
        )
        scores = nt_dot(queries, keys) * inv_scale + shut
        top = jnp.max(scores, axis=1, keepdims=True)
        terms = jnp.exp(scores - top)
        total = jnp.sum(terms, axis=1, keepdims=True)
        mixed = jnp.dot(terms.astype(BF16), values, preferred_element_type=F32) / total
        for h in range(GROUP):
            head = group * GROUP + h
            out_ref[:, head * HD : (head + 1) * HD] = (mixed[h * rows : (h + 1) * rows] * keep).astype(BF16)


def final_kernel(attended_ref, gate_ref, gain_ref, y0, y1, y2, y3, out_ref, gated):
    me = lax.axis_index("head")
    rows, width = y0.shape
    heads_width = attended_ref.shape[1]
    out_ref[:, :heads_width] = attended_ref[...]
    squares = jnp.zeros((rows, 1), F32)
    for hop, ref in enumerate((y0, y1, y2, y3)):
        gate = columns(gate_ref, me ^ hop, width).astype(F32)
        part = ref[...].astype(F32) * (gate / (1.0 + jnp.exp(-gate)))
        gated[:, hop * width : (hop + 1) * width] = part
        squares = squares + jnp.sum(part * part, axis=1, keepdims=True)
    scale = lax.rsqrt(squares / MI + EPSILON)
    for hop in range(4):
        gain = columns(gain_ref, me ^ hop, width)
        part = gated[:, hop * width : (hop + 1) * width] * scale * gain
        start = pl.multiple_of(heads_width + (me ^ hop) * width, LANES)
        out_ref[:, pl.ds(start, width)] = part.astype(BF16)


def hopped(block, hop):
    return lax.ppermute(block, "head", [(i, i ^ hop) for i in range(4)])


def local(
    queries,
    fresh_keyvals,
    ssm_input,
    gate_input,
    state_maps,
    step_logit,
    slot_mask,
    cache_pool,
    page_map,
    cached_lengths,
    prior_state,
    decay_log,
    step_bias,
    skip_gain,
    norm_gain,
):
    rows = ssm_input.shape[0]
    width = MI // 4
    small_width = state_maps.shape[1] + LANES
    small, x1, x2, x3 = call(
        pack_kernel,
        [((rows, small_width), BF16)] + [((rows, width), BF16)] * 3,
        [VMEM] * 4,
    )(ssm_input, state_maps, step_logit, slot_mask.reshape(1, rows))
    small2 = hopped(small, 2)
    small1 = hopped(small, 1)
    x2 = hopped(x2, 2)
    x3 = hopped(x3, 3)
    x1 = hopped(x1, 1)
    kv2 = hopped(fresh_keyvals, 2)
    kv1 = hopped(fresh_keyvals, 1)
    small3 = hopped(small2, 1)
    kv3 = hopped(kv2, 1)

    slots, half = cache_pool.shape[0], cache_pool.shape[1]
    copies = jnp.broadcast_to(cache_pool[:, None], (slots, 4, half, 2 * HD)).reshape(slots * 4 * half, 2 * HD)
    pages = lax.all_to_all(copies, ("dp", "head"), split_axis=0, concat_axis=0, tiled=True)

    span = 4 * rows
    y0, y1, y2, y3 = call(
        scan_kernel,
        [((rows, width), BF16)] * 4,
        [SMEM] * 3 + [VMEM] * 9,
        [pltpu.VMEM((span, small_width), BF16), pltpu.VMEM((span, width), BF16), pltpu.VMEM((span, width), BF16)],
    )(
        decay_log, step_bias, skip_gain,
        small, small1, small2, small3, ssm_input, x1, x2, x3, prior_state,
    )
    y2 = hopped(y2, 2)
    y3 = hopped(y3, 3)
    y1 = hopped(y1, 1)
    (attended,) = call(
        attention_kernel, [((rows, QH * HD), BF16)], [SMEM] * 2 + [VMEM] * 10
    )(
        page_map, cached_lengths, queries, pages,
        fresh_keyvals, kv1, kv2, kv3, small, small1, small2, small3,
    )
    (result,) = call(
        final_kernel,
        [((rows, QH * HD + MI), BF16)],
        [VMEM] * 7,
        [pltpu.VMEM((rows, MI), F32)],
    )(attended, gate_input, norm_gain.reshape(1, MI), y0, y1, y2, y3)
    return result


def solution(mesh):
    in_specs = (
        P(("dp", "head"), None),
        P(("dp", "head"), None),
        P(("dp", "head"), None),
        P(("dp", "head"), None),
        P(("dp", "head"), None),
        P(("dp", "head"), None),
        P(("dp", "head")),
        P("dp", "head", None),
        P("dp", None),
        P("dp"),
        P("dp", "head", None, None),
        P("head"),
        P("head"),
        P("head"),
        P(),
    )
    out_specs = P(("dp", "head"), None)
    return jax.shard_map(local, mesh=mesh, in_specs=in_specs, out_specs=out_specs, check_vma=False)
```

```python
import math

import jax
import jax.numpy as jnp
from jax import lax
from jax.experimental import pallas as pl
from jax.experimental.pallas import tpu as pltpu
from jax.sharding import PartitionSpec as P

HD = 128
QH = 12
KVH = 2
GROUP = QH // KVH
STATE = 256
MI = 3072
PAGE = 16
LANES = 128
EPSILON = 1e-05
BF16 = jnp.bfloat16
F32 = jnp.float32
HIGHEST = lax.Precision.HIGHEST
VMEM = pl.BlockSpec(memory_space=pltpu.VMEM)
SMEM = pl.BlockSpec(memory_space=pltpu.SMEM)
ANY = pl.BlockSpec(memory_space=pl.ANY)
MAPS = 2 * STATE
NOTES = slice(MAPS, MAPS + LANES)
TOLD = MAPS + LANES
KEYVALS = 2 * KVH * HD
MASK_LANE = 24
PARAM_LANE = 32
ALL_HEADS = 24


def call(kernel, outs, specs, scratch=(), limit=24):
    return pl.pallas_call(
        kernel,
        out_shape=[jax.ShapeDtypeStruct(shape, dtype) for shape, dtype in outs],
        in_specs=specs,
        out_specs=[VMEM] * len(outs),
        scratch_shapes=list(scratch),
        compiler_params=pltpu.CompilerParams(vmem_limit_bytes=limit << 20),
    )


def columns(ref, owner, width):
    return ref[:, pl.ds(pl.multiple_of(owner * width, LANES), width)]


def iota(shape, dim):
    return lax.broadcasted_iota(jnp.int32, shape, dim)


def rolled(array, first, axis):
    size = array.shape[axis]
    return pltpu.roll(array, lax.rem(size - first, size), axis)


def nt_dot(a, b, precision=None):
    return lax.dot_general(
        a, b, (((1,), (1,)), ((), ())), preferred_element_type=F32, precision=precision
    )


def pack_kernel(
    log_rate_ref, bias_ref, skip_ref, x_ref, maps_ref, logit_ref, mask_ref, keyval_ref, told_ref, far_ref,
):
    me = lax.axis_index("head")
    rows, width = x_ref.shape[0], x_ref.shape[1] // 4
    far_ref[:, :width] = columns(x_ref, me ^ 2, width)
    far_ref[:, width : 2 * width] = columns(x_ref, me ^ 3, width)
    far_ref[:, 2 * width :] = keyval_ref[...]
    told_ref[:, :MAPS] = maps_ref[...]
    heads, head_count = logit_ref.shape[0], log_rate_ref.shape[0]
    pick = (iota((heads, LANES), 0) == iota((heads, LANES), 1)).astype(F32).astype(BF16)
    notes = lax.dot_general(logit_ref[...], pick, (((0,), (0,)), ((), ())), preferred_element_type=F32)
    diagonal = iota((rows, rows), 0) == iota((rows, rows), 1)
    real = jnp.broadcast_to(mask_ref[...], (rows, rows)) > 0
    real = jnp.sum(jnp.where(diagonal & real, 1.0, 0.0), axis=1, keepdims=True)
    lane, row = iota((1, LANES), 1), iota((rows, 1), 0)
    params = jnp.zeros((rows, LANES), F32)
    for kind, ref in enumerate((log_rate_ref, bias_ref, skip_ref)):
        value = jnp.zeros((1, LANES), F32)
        for head in range(head_count):
            value = jnp.where(lane == PARAM_LANE + me * head_count + head, ref[head], value)
        high = value.astype(BF16).astype(F32)
        middle = (value - high).astype(BF16).astype(F32)
        for part, piece in enumerate((high, middle, value - high - middle)):
            params = jnp.where(row == 3 * kind + part, piece, params)
    in_params = (lane >= PARAM_LANE) & (lane < PARAM_LANE + ALL_HEADS)
    notes = jnp.where(lane < heads, notes, jnp.where(in_params, params, real))
    told_ref[:, NOTES] = notes.astype(BF16)


def order_kernel(pool_ref, even_ref, odd_ref):
    request = lax.axis_index("dp")
    half_slots = even_ref.shape[0]

    def place(at, carry):
        distance, rest, bit = 0, at, half_slots
        while bit > 1:
            distance, rest, bit = distance + (rest % 2) * bit, rest // 2, bit // 2
        even_ref[at] = pool_ref[request ^ distance]
        odd_ref[at] = pool_ref[request ^ distance ^ 1]
        return carry

    lax.fori_loop(0, half_slots, place, 0, unroll=half_slots <= 8)


def copy_kernel(from_ref, to_ref):
    to_ref[...] = from_ref[...]


def token_at(index, rows, me):
    return (me ^ (index // rows)) * rows + index % rows


def head_sums(tolds, me):
    rows = tolds[0].shape[0]
    span = 4 * rows
    notes = jnp.concatenate([ref[:, NOTES] for ref in tolds], axis=0)
    params = sum(ref[0:16, NOTES].astype(F32) for ref in tolds).astype(BF16)
    head, lane = iota((32, LANES), 0), iota((32, LANES), 1)
    by_row = jnp.where(head == lane, 1.0, 0.0).astype(BF16)
    by_row_params = jnp.where(head + PARAM_LANE == lane, 1.0, 0.0).astype(BF16)
    source, target = iota((LANES, LANES), 0), iota((LANES, LANES), 1)
    by_lane_params = jnp.where((source == target + PARAM_LANE) & (target < ALL_HEADS), 1.0, 0.0).astype(BF16)
    row_params = nt_dot(by_row_params, params)
    lane_params = jnp.dot(params, by_lane_params, preferred_element_type=F32)

    def row_param(kind):
        return sum(row_params[:, 3 * kind + part : 3 * kind + part + 1] for part in range(3))

    def lane_param(kind):
        return sum(lane_params[3 * kind + part : 3 * kind + part + 1, :] for part in range(3))

    row_logits = nt_dot(by_row, notes)
    lane_logits = notes.astype(F32)
    row_mask = row_logits[MASK_LANE : MASK_LANE + 1, :]
    lane_mask = lane_logits[:, MASK_LANE : MASK_LANE + 1]
    row_steps = jnp.log(1.0 + jnp.exp(row_logits + row_param(1))) * row_mask
    lane_steps = jnp.log(1.0 + jnp.exp(lane_logits + lane_param(1))) * lane_mask
    token = token_at(iota((span, span), 0), rows, me)
    source = token_at(iota((span, span), 1), rows, me)
    upto = jnp.where(source <= token, 1.0, 0.0)
    row_sum = nt_dot(-jnp.exp(row_param(0)) * row_steps, upto, HIGHEST)
    lane_sum = jnp.dot(upto, -jnp.exp(lane_param(0)) * lane_steps, preferred_element_type=F32, precision=HIGHEST)
    return row_sum - jnp.log(row_steps), lane_sum, lane_param(2), lane_mask


def remote_kernel(
    told0, told1, told2, told3, x0_ref, x1_ref, prior_ref,
    y_ref, shift_ref, total_ref, skip_ref,
):
    me = lax.axis_index("head")
    rows, width = told0.shape[0], y_ref.shape[1]
    near, head_count = 2 * rows, width // HD
    shift, total, skip, mask = head_sums((told0, told1, told2, told3), me)
    shift_ref[...] = shift
    total_ref[...] = total
    skip_ref[...] = jnp.broadcast_to(skip, skip_ref.shape)
    own_shift = rolled(shift, me * head_count, 0)
    own_total = rolled(total, me * head_count, 1)
    in_map = jnp.concatenate([told0[:, :STATE], told1[:, :STATE]], axis=0)
    out_map = jnp.concatenate([told2[:, STATE:MAPS], told3[:, STATE:MAPS]], axis=0)
    products = nt_dot(out_map, in_map)
    from_prior = nt_dot(out_map, prior_ref[0].reshape(width, STATE))
    x = jnp.concatenate([columns(x0_ref, me, width), columns(x1_ref, me, width)], axis=0)
    earlier = jnp.where(jnp.broadcast_to(me, (near, near)) < 2, 0.0, -jnp.inf)
    for head in range(head_count):
        cols = slice(head * HD, (head + 1) * HD)
        sums = own_total[near:, head : head + 1]
        weights = (jnp.exp(sums - own_shift[head : head + 1, :near] + earlier) * products).astype(BF16)
        y = jnp.dot(weights, x[:, cols], preferred_element_type=F32) + from_prior[:, cols] * jnp.exp(sums)
        y_ref[:, cols] = (y * mask[near:]).astype(BF16)


def near_kernel(
    shift_ref, total_ref, skip_ref, told0, told1, told2, told3, x0_ref, x1_ref, far_ref, relayed_ref,
    prior0_ref, prior1_ref, y_ref,
):
    me = lax.axis_index("head")
    rows, width = told0.shape[0], x0_ref.shape[1] // 4
    near, span, head_count = 2 * rows, 4 * rows, width // HD
    in_map = jnp.concatenate([ref[:, :STATE] for ref in (told0, told1, told2, told3)], axis=0)
    out_map = told0[:, STATE:MAPS]
    products = nt_dot(out_map, in_map)
    token = token_at(iota((rows, span), 0), rows, me)
    source = token_at(iota((rows, span), 1), rows, me)
    causal = jnp.where(source <= token, 0.0, -jnp.inf)
    mask = told0[:, MAPS + MASK_LANE : MAPS + MASK_LANE + 1].astype(F32)
    shift, total, skip = shift_ref[...], total_ref[:rows, :], skip_ref[...]
    for hop in range(4):
        block = me ^ hop
        block_shift = rolled(shift, block * head_count, 0)
        block_total = rolled(total, block * head_count, 1)
        block_skip = rolled(skip, block * head_count, 1)[0:1, :]
        own = columns(x0_ref, block, width)
        sources = [own, columns(x1_ref, block, width)]
        reach = near
        if hop < 2:
            reach = span
            place = (hop, 1 - hop)
            sources += [ref[:, at * width : (at + 1) * width] for ref, at in zip((far_ref, relayed_ref), place)]
            from_prior = nt_dot(out_map, (prior0_ref, prior1_ref)[hop][0].reshape(width, STATE))
        sources = jnp.concatenate(sources, axis=0)
        for head in range(head_count):
            cols = slice(head * HD, (head + 1) * HD)
            sums = block_total[:, head : head + 1]
            weights = jnp.exp(sums - block_shift[head : head + 1, :reach] + causal[:, :reach]) * products[:, :reach]
            y = jnp.dot(weights.astype(BF16), sources[:, cols], preferred_element_type=F32)
            y = y + block_skip[:, head : head + 1] * own[:, cols].astype(F32)
            if hop < 2:
                y = y + from_prior[:, cols] * jnp.exp(sums)
            y_ref[:, hop * width + head * HD : hop * width + (head + 1) * HD] = y * mask


def attention_kernel(
    page_map_ref, length_ref, query_ref, pages0, pages1,
    kv0, kv1, far_ref, relayed_ref, told0, told1, told2, told3, out_ref,
):
    me = lax.axis_index("head")
    request = lax.axis_index("dp")
    rows = query_ref.shape[0]
    slots, half = pages0.shape[1], pages0.shape[2]
    part = slots * half
    cached = 2 * part
    inv_scale = 1.0 / math.sqrt(HD)
    lane = iota((1, cached), 1)

    def place(page, base):
        return jnp.where(lane % part // half == (page_map_ref[0, page] ^ request), page * PAGE, base)

    position = lax.fori_loop(0, slots, place, jnp.zeros((1, cached), jnp.int32), unroll=slots <= 8)
    position = position + ((me ^ (lane // part)) % 2) * half + lane % half
    shut = [jnp.broadcast_to(jnp.where(position < length_ref[0], 0.0, -jnp.inf), (rows, cached))]
    ones = jnp.where(iota((8, LANES), 1) == MASK_LANE, 1.0, 0.0).astype(BF16)
    token, source = iota((rows, rows), 0), iota((rows, rows), 1)
    for hop, ref in enumerate((told0, told1, told2, told3)):
        real = nt_dot(ones, ref[:, NOTES])[0:1, :] > 0.5
        limit = token if hop == 0 else jnp.where((me ^ hop) < me, rows, -1)
        shut.append(jnp.where(real & (source <= limit), 0.0, -jnp.inf))
    shut = jnp.concatenate(shut, axis=1)
    shut = jnp.concatenate([shut] * GROUP, axis=0)
    keep = told0[:, MAPS + MASK_LANE : MAPS + MASK_LANE + 1].astype(F32)
    pages = [ref[chip].reshape(part, 2 * HD) for chip in range(2) for ref in (pages0, pages1)]
    for group in range(KVH):
        queries = jnp.concatenate(
            [query_ref[:, (group * GROUP + h) * HD : (group * GROUP + h + 1) * HD] for h in range(GROUP)],
            axis=0,
        )
        here = jnp.broadcast_to(me // 2, (part, 2 * HD)) == group
        old = [jnp.where(here, pages[core], pages[core ^ 2]) for core in range(2)]
        base = 2 * group * HD
        fresh = []
        for ref in (kv0, kv1, far_ref, relayed_ref):
            start = ref.shape[1] - KEYVALS + base
            fresh.append(ref[:, start : start + 2 * HD])
        every = jnp.concatenate(old + fresh, axis=0)
        keys, values = every[:, :HD], every[:, HD:]
        scores = nt_dot(queries, keys) * inv_scale + shut
        top = jnp.max(scores, axis=1, keepdims=True)
        terms = jnp.exp(scores - top)
        total = jnp.sum(terms, axis=1, keepdims=True)
        mixed = jnp.dot(terms.astype(BF16), values, preferred_element_type=F32) / total
        for h in range(GROUP):
            head = group * GROUP + h
            out_ref[:, head * HD : (head + 1) * HD] = (mixed[h * rows : (h + 1) * rows] * keep).astype(BF16)


def final_kernel(attended_ref, gate_ref, gain_ref, y_ref, y2_ref, y3_ref, out_ref, gated):
    me = lax.axis_index("head")
    rows, width = y_ref.shape[0], y2_ref.shape[1]
    heads_width = attended_ref.shape[1]
    out_ref[:, :heads_width] = attended_ref[...]
    squares = jnp.zeros((rows, 1), F32)
    for hop, far in enumerate((None, None, y2_ref[:rows, :], y3_ref[rows:, :])):
        gate = columns(gate_ref, me ^ hop, width).astype(F32)
        part = y_ref[:, hop * width : (hop + 1) * width]
        if far is not None:
            part = part + far.astype(F32)
        part = part.astype(BF16).astype(F32) * (gate / (1.0 + jnp.exp(-gate)))
        gated[:, hop * width : (hop + 1) * width] = part
        squares = squares + jnp.sum(part * part, axis=1, keepdims=True)
    scale = lax.rsqrt(squares / MI + EPSILON)
    for hop in range(4):
        gain = columns(gain_ref, me ^ hop, width)
        part = gated[:, hop * width : (hop + 1) * width] * scale * gain
        start = pl.multiple_of(heads_width + (me ^ hop) * width, LANES)
        out_ref[:, pl.ds(start, width)] = part.astype(BF16)


def behind(block, earlier):
    return block if earlier is None else lax.optimization_barrier((block, earlier))[0]


def hopped(block, hop):
    return lax.ppermute(block, "head", [(i, i ^ hop) for i in range(4)])


def local(
    queries,
    fresh_keyvals,
    ssm_input,
    gate_input,
    state_maps,
    step_logit,
    slot_mask,
    cache_pool,
    page_map,
    cached_lengths,
    prior_state,
    decay_log,
    step_bias,
    skip_gain,
    norm_gain,
):
    rows = ssm_input.shape[0]
    width = MI // 4
    slots, half = cache_pool.shape[0], cache_pool.shape[1]
    pages, sent = call(order_kernel, [((slots // 2, half, 2 * HD), BF16)] * 2, [VMEM])(cache_pool)
    told, far = call(
        pack_kernel,
        [((rows, TOLD), BF16), ((rows, 2 * width + KEYVALS), BF16)],
        [SMEM] * 3 + [VMEM] * 5,
        limit=60,
    )(
        decay_log, step_bias, skip_gain,
        ssm_input, behind(state_maps, sent), step_logit.T, slot_mask.reshape(1, rows), fresh_keyvals,
    )
    prior1 = hopped(prior_state, 1)
    x1 = hopped(ssm_input, 1)
    kv1 = hopped(fresh_keyvals, 1)
    told1 = hopped(told, 1)
    told2 = hopped(told, 2)
    far = hopped(far, 2)
    told3 = hopped(told2, 1)
    (prior0,) = call(copy_kernel, [(prior_state.shape, BF16)], [VMEM])(behind(prior_state, told1))

    parts, bit, came, earlier = [pages], 1, None, None
    while bit < slots:
        if bit > 1:
            keep = parts[0].shape[0] // 2
            sent = jnp.concatenate([part[keep:] for part in parts])
            parts = [part[:keep] for part in parts]
        if bit == 2:
            sent = behind(sent, told1)
        if 2 * bit == slots:
            sent = behind(sent, prior0)
        came, earlier = lax.ppermute(sent, "dp", [(i, i ^ bit) for i in range(slots)]), came
        keep = parts[0].shape[0]
        parts = parts + [came[i * keep : (i + 1) * keep] for i in range(len(parts))]
        bit *= 2
    pages = jnp.concatenate(parts)

    y2, shift, total, skip = call(
        remote_kernel,
        [((2 * rows, width), BF16), ((32, 4 * rows), F32), ((4 * rows, LANES), F32), ((8, LANES), F32)],
        [VMEM] * 7,
    )(told, told1, told2, behind(behind(told3, earlier), prior1), ssm_input, x1, prior0)
    relayed = hopped(behind(far, y2), 1)
    pages = jnp.stack([pages, hopped(pages, 2)])
    pages1 = hopped(pages, 1)
    y2 = hopped(y2, 2)
    y3 = hopped(y2, 1)
    (y,) = call(near_kernel, [((rows, MI), F32)], [VMEM] * 13)(
        shift, total, skip, told, told1, told2, told3, ssm_input, x1, far, relayed, prior0, prior1
    )
    (attended,) = call(attention_kernel, [((rows, QH * HD), BF16)], [SMEM] * 2 + [VMEM] * 11)(
        page_map, cached_lengths, queries, pages, pages1,
        fresh_keyvals, kv1, far, relayed, told, told1, told2, told3,
    )
    (result,) = call(
        final_kernel,
        [((rows, QH * HD + MI), BF16)],
        [VMEM] * 6,
        [pltpu.VMEM((rows, MI), F32)],
    )(attended, gate_input, norm_gain.reshape(1, MI), y, y2, y3)
    return result


def solution(mesh):
    in_specs = (
        P(("dp", "head"), None),
        P(("dp", "head"), None),
        P(("dp", "head"), None),
        P(("dp", "head"), None),
        P(("dp", "head"), None),
        P(("dp", "head"), None),
        P(("dp", "head")),
        P("dp", "head", None),
        P("dp", None),
        P("dp"),
        P("dp", "head", None, None),
        P("head"),
        P("head"),
        P("head"),
        P(),
    )
    out_specs = P(("dp", "head"), None)
    return jax.shard_map(local, mesh=mesh, in_specs=in_specs, out_specs=out_specs, check_vma=False)
```

```python
import math

import jax
import jax.numpy as jnp
from jax import lax
from jax.experimental import pallas as pl
from jax.experimental.pallas import tpu as pltpu
from jax.sharding import PartitionSpec as P

HD = 128
QH = 12
KVH = 2
GROUP = QH // KVH
STATE = 256
MI = 3072
PAGE = 16
LANES = 128
EPSILON = 1e-05
BF16 = jnp.bfloat16
F32 = jnp.float32
HIGHEST = lax.Precision.HIGHEST
VMEM = pl.BlockSpec(memory_space=pltpu.VMEM)
SMEM = pl.BlockSpec(memory_space=pltpu.SMEM)
ANY = pl.BlockSpec(memory_space=pl.ANY)
NOTES = slice(STATE, STATE + LANES)
AHEAD = STATE + LANES
IN_MAP = slice(AHEAD, AHEAD + STATE)
TOLD = AHEAD + STATE
KEYVALS = 2 * KVH * HD
MASK_LANE = 24
PARAM_LANE = 32
ALL_HEADS = 24


def call(kernel, outs, specs, scratch=(), limit=24):
    return pl.pallas_call(
        kernel,
        out_shape=[jax.ShapeDtypeStruct(shape, dtype) for shape, dtype in outs],
        in_specs=specs,
        out_specs=[VMEM] * len(outs),
        scratch_shapes=list(scratch),
        compiler_params=pltpu.CompilerParams(vmem_limit_bytes=limit << 20),
    )


def columns(ref, owner, width):
    return ref[:, pl.ds(pl.multiple_of(owner * width, LANES), width)]


def iota(shape, dim):
    return lax.broadcasted_iota(jnp.int32, shape, dim)


def rolled(array, first, axis):
    size = array.shape[axis]
    return pltpu.roll(array, lax.rem(size - first, size), axis)


def nt_dot(a, b, precision=None):
    return lax.dot_general(
        a, b, (((1,), (1,)), ((), ())), preferred_element_type=F32, precision=precision
    )


def pack_kernel(
    log_rate_ref, bias_ref, skip_ref, x_ref, maps_ref, logit_ref, mask_ref, keyval_ref, told_ref, ahead_ref, far_ref,
):
    me = lax.axis_index("head")
    rows, width = x_ref.shape[0], x_ref.shape[1] // 4
    far_ref[:, :width] = columns(x_ref, me ^ 2, width)
    far_ref[:, width : 2 * width] = columns(x_ref, me ^ 3, width)
    far_ref[:, 2 * width : 2 * width + STATE] = maps_ref[:, :STATE]
    far_ref[:, 2 * width + STATE :] = keyval_ref[...]
    told_ref[:, IN_MAP] = maps_ref[:, :STATE]
    told_ref[:, :STATE] = maps_ref[:, STATE:]
    ahead_ref[:, :STATE] = maps_ref[:, STATE:]
    heads, head_count = logit_ref.shape[0], log_rate_ref.shape[0]
    pick = (iota((heads, LANES), 0) == iota((heads, LANES), 1)).astype(F32).astype(BF16)
    notes = lax.dot_general(logit_ref[...], pick, (((0,), (0,)), ((), ())), preferred_element_type=F32)
    diagonal = iota((rows, rows), 0) == iota((rows, rows), 1)
    real = jnp.broadcast_to(mask_ref[...], (rows, rows)) > 0
    real = jnp.sum(jnp.where(diagonal & real, 1.0, 0.0), axis=1, keepdims=True)
    lane, row = iota((1, LANES), 1), iota((rows, 1), 0)
    params = jnp.zeros((rows, LANES), F32)
    for kind, ref in enumerate((log_rate_ref, bias_ref, skip_ref)):
        value = jnp.zeros((1, LANES), F32)
        for head in range(head_count):
            value = jnp.where(lane == PARAM_LANE + me * head_count + head, ref[head], value)
        high = value.astype(BF16).astype(F32)
        middle = (value - high).astype(BF16).astype(F32)
        for part, piece in enumerate((high, middle, value - high - middle)):
            params = jnp.where(row == 3 * kind + part, piece, params)
    in_params = (lane >= PARAM_LANE) & (lane < PARAM_LANE + ALL_HEADS)
    notes = jnp.where(lane < heads, notes, jnp.where(in_params, params, real))
    told_ref[:, NOTES] = notes.astype(BF16)
    ahead_ref[:, NOTES] = notes.astype(BF16)


def order_kernel(pool_ref, far_pool_ref, even_ref, odd_ref):
    request = lax.axis_index("dp")
    half_slots = even_ref.shape[0]

    def place(at, carry):
        distance, rest, bit = 0, at, half_slots
        while bit > 1:
            distance, rest, bit = distance + (rest % 2) * bit, rest // 2, bit // 2
        for chip, ref in enumerate((pool_ref, far_pool_ref)):
            even_ref[at, chip] = ref[request ^ distance]
            odd_ref[at, chip] = ref[request ^ distance ^ 1]
        return carry

    lax.fori_loop(0, half_slots, place, 0, unroll=half_slots <= 8)


def token_at(index, rows, me):
    return (me ^ (index // rows)) * rows + index % rows


def head_sums(tolds, me):
    rows = tolds[0].shape[0]
    span = 4 * rows
    notes = jnp.concatenate([ref[:, NOTES] for ref in tolds], axis=0)
    params = sum(ref[0:16, NOTES].astype(F32) for ref in tolds).astype(BF16)
    head, lane = iota((32, LANES), 0), iota((32, LANES), 1)
    by_row = jnp.where(head == lane, 1.0, 0.0).astype(BF16)
    by_row_params = jnp.where(head + PARAM_LANE == lane, 1.0, 0.0).astype(BF16)
    row_params = nt_dot(by_row_params, params)
    source, target = iota((LANES, LANES), 0), iota((LANES, LANES), 1)
    by_lane_params = jnp.where((source == target + PARAM_LANE) & (target < ALL_HEADS), 1.0, 0.0).astype(BF16)
    skips = jnp.dot(params, by_lane_params, preferred_element_type=F32)
    skip = skips[6:7, :] + skips[7:8, :] + skips[8:9, :]

    def row_param(kind):
        return sum(row_params[:, 3 * kind + part : 3 * kind + part + 1] for part in range(3))

    logits = nt_dot(by_row, notes)
    steps = jnp.log(1.0 + jnp.exp(logits + row_param(1))) * logits[MASK_LANE : MASK_LANE + 1, :]
    token = token_at(iota((span, span), 0), rows, me)
    source = token_at(iota((span, span), 1), rows, me)
    upto = jnp.where(source <= token, 1.0, 0.0)
    sums = nt_dot(-jnp.exp(row_param(0)) * steps, upto, HIGHEST)
    by_token = jnp.concatenate([sums] * (LANES // 32), axis=0).T
    return sums - jnp.log(steps), by_token, skip


def remote_kernel(
    told0, told1, ahead2, ahead3, x0_ref, x1_ref, prior1_ref,
    y_ref, shift_ref, total_ref, skip_ref,
):
    me = lax.axis_index("head")
    rows, width = told0.shape[0], y_ref.shape[1]
    near, head_count = 2 * rows, width // HD
    shift, total, skip = head_sums((told0, told1, ahead2, ahead3), me)
    shift_ref[...] = shift
    total_ref[...] = total
    skip_ref[...] = jnp.broadcast_to(skip, skip_ref.shape)
    block = me ^ 1
    block_shift = rolled(shift, block * head_count, 0)
    block_total = rolled(total[near:], block * head_count, 1)
    mask = jnp.concatenate([ref[:, STATE + MASK_LANE : STATE + MASK_LANE + 1] for ref in (ahead2, ahead3)], axis=0)
    mask = mask.astype(F32)
    out_map = jnp.concatenate([ahead2[:, :STATE], ahead3[:, :STATE]], axis=0)
    from_prior = nt_dot(out_map, prior1_ref[0].reshape(width, STATE))

    def write(from_x):
        for head in range(head_count):
            cols = slice(head * HD, (head + 1) * HD)
            sums = block_total[:, head : head + 1]
            y = from_prior[:, cols] * jnp.exp(sums)
            if from_x is not None:
                y = y + from_x(cols, sums - block_shift[head : head + 1, :near])
            y_ref[:, cols] = (y * mask).astype(BF16)

    @pl.when(me < 2)
    def _():
        in_map = jnp.concatenate([told0[:, IN_MAP], told1[:, IN_MAP]], axis=0)
        products = nt_dot(out_map, in_map)
        x = jnp.concatenate([columns(x0_ref, block, width), columns(x1_ref, block, width)], axis=0)

        def from_x(cols, gaps):
            return jnp.dot((jnp.exp(gaps) * products).astype(BF16), x[:, cols], preferred_element_type=F32)

        write(from_x)

    @pl.when(me >= 2)
    def _():
        write(None)


def near_kernel(
    shift_ref, total_ref, skip_ref, told0, told1, x0_ref, x1_ref, far_ref, relayed_ref,
    prior0_ref, prior1_ref, y_ref,
):
    me = lax.axis_index("head")
    rows, width = told0.shape[0], x0_ref.shape[1] // 4
    near, span, head_count = 2 * rows, 4 * rows, width // HD
    far_map = slice(2 * width, 2 * width + STATE)
    out_map = told0[:, :STATE]
    mask = told0[:, STATE + MASK_LANE : STATE + MASK_LANE + 1].astype(F32)
    shift, total, skip = shift_ref[...], total_ref[:rows, :], skip_ref[...]

    def write(with_far):
        whole = span if with_far else near
        in_map = [told0[:, IN_MAP], told1[:, IN_MAP]]
        if with_far:
            in_map += [far_ref[:, far_map], relayed_ref[:, far_map]]
        products = nt_dot(out_map, jnp.concatenate(in_map, axis=0))
        token = token_at(iota((rows, whole), 0), rows, me)
        source = token_at(iota((rows, whole), 1), rows, me)
        causal = jnp.where(source <= token, 0.0, -jnp.inf)
        for hop in range(4):
            block = me ^ hop
            block_shift = rolled(shift, block * head_count, 0)
            block_total = rolled(total, block * head_count, 1)
            block_skip = rolled(skip, block * head_count, 1)[0:1, :]
            own = columns(x0_ref, block, width)
            sources = [own, columns(x1_ref, block, width)]
            reach = near
            if hop < 2:
                reach = whole
                from_prior = nt_dot(out_map, (prior0_ref, prior1_ref)[hop][0].reshape(width, STATE))
            if reach == span:
                place = (hop, 1 - hop)
                sources += [ref[:, at * width : (at + 1) * width] for ref, at in zip((far_ref, relayed_ref), place)]
            sources = jnp.concatenate(sources, axis=0)
            for head in range(head_count):
                cols = slice(head * HD, (head + 1) * HD)
                sums = block_total[:, head : head + 1]
                weights = jnp.exp(sums - block_shift[head : head + 1, :reach] + causal[:, :reach]) * products[:, :reach]
                y = jnp.dot(weights.astype(BF16), sources[:, cols], preferred_element_type=F32)
                y = y + block_skip[:, head : head + 1] * own[:, cols].astype(F32)
                if hop < 2:
                    y = y + from_prior[:, cols] * jnp.exp(sums)
                y_ref[:, hop * width + head * HD : hop * width + (head + 1) * HD] = y * mask

    @pl.when(me < 2)
    def _():
        write(False)

    @pl.when(me >= 2)
    def _():
        write(True)


def attention_kernel(
    page_map_ref, length_ref, query_ref, pages0, pages1,
    kv0, kv1, far_ref, relayed_ref, told0, told1, told2, told3, out_ref,
):
    me = lax.axis_index("head")
    request = lax.axis_index("dp")
    rows = query_ref.shape[0]
    slots, half = pages0.shape[0], pages0.shape[2]
    part = slots * half
    cached = 2 * part
    inv_scale = 1.0 / math.sqrt(HD)
    lane = iota((1, cached), 1)

    def place(page, base):
        return jnp.where(lane % part // half == (page_map_ref[0, page] ^ request), page * PAGE, base)

    position = lax.fori_loop(0, slots, place, jnp.zeros((1, cached), jnp.int32), unroll=slots <= 8)
    position = position + ((me ^ (lane // part)) % 2) * half + lane % half
    old_shut = jnp.broadcast_to(jnp.where(position < length_ref[0], 0.0, -jnp.inf), (rows, cached))
    ones = jnp.where(iota((8, LANES), 1) == MASK_LANE, 1.0, 0.0).astype(BF16)
    token, source = iota((rows, rows), 0), iota((rows, rows), 1)
    keep = told0[:, STATE + MASK_LANE : STATE + MASK_LANE + 1].astype(F32)
    pages = [ref[:, chip].reshape(part, 2 * HD) for chip in range(2) for ref in (pages0, pages1)]

    def write(reach):
        shut = [old_shut]
        for hop, ref in enumerate((told0, told1, told2, told3)[:reach]):
            real = nt_dot(ones, ref[:, NOTES])[0:1, :] > 0.5
            limit = token if hop == 0 else jnp.where((me ^ hop) < me, rows, -1)
            shut.append(jnp.where(real & (source <= limit), 0.0, -jnp.inf))
        shut = jnp.concatenate(shut, axis=1)
        shut = jnp.concatenate([shut] * GROUP, axis=0)
        for group in range(KVH):
            queries = jnp.concatenate(
                [query_ref[:, (group * GROUP + h) * HD : (group * GROUP + h + 1) * HD] for h in range(GROUP)],
                axis=0,
            )
            here = jnp.broadcast_to(me // 2, (part, 2 * HD)) == group
            every = [jnp.where(here, pages[core], pages[core ^ 2]) for core in range(2)]
            for ref in (kv0, kv1, far_ref, relayed_ref)[:reach]:
                start = ref.shape[1] - KEYVALS + 2 * group * HD
                every.append(ref[:, start : start + 2 * HD])
            every = jnp.concatenate(every, axis=0)
            keys, values = every[:, :HD], every[:, HD:]
            scores = nt_dot(queries, keys) * inv_scale + shut
            top = jnp.max(scores, axis=1, keepdims=True)
            terms = jnp.exp(scores - top)
            total = jnp.sum(terms, axis=1, keepdims=True)
            mixed = jnp.dot(terms.astype(BF16), values, preferred_element_type=F32) / total
            for h in range(GROUP):
                head = group * GROUP + h
                out_ref[:, head * HD : (head + 1) * HD] = (mixed[h * rows : (h + 1) * rows] * keep).astype(BF16)

    @pl.when(me < 2)
    def _():
        write(2)

    @pl.when(me >= 2)
    def _():
        write(4)


def final_kernel(attended_ref, gate_ref, gain_ref, y_ref, y2_ref, y3_ref, out_ref, gated):
    me = lax.axis_index("head")
    rows, width = y_ref.shape[0], y2_ref.shape[1]
    heads_width = attended_ref.shape[1]
    out_ref[:, :heads_width] = attended_ref[...]
    squares = jnp.zeros((rows, 1), F32)
    for hop, far in enumerate((None, None, y3_ref[rows:, :], y2_ref[:rows, :])):
        gate = columns(gate_ref, me ^ hop, width).astype(F32)
        part = y_ref[:, hop * width : (hop + 1) * width]
        if far is not None:
            part = part + far.astype(F32)
        part = part.astype(BF16).astype(F32) * (gate / (1.0 + jnp.exp(-gate)))
        gated[:, hop * width : (hop + 1) * width] = part
        squares = squares + jnp.sum(part * part, axis=1, keepdims=True)
    scale = lax.rsqrt(squares / MI + EPSILON)
    for hop in range(4):
        gain = columns(gain_ref, me ^ hop, width)
        part = gated[:, hop * width : (hop + 1) * width] * scale * gain
        start = pl.multiple_of(heads_width + (me ^ hop) * width, LANES)
        out_ref[:, pl.ds(start, width)] = part.astype(BF16)


def behind(block, earlier):
    return lax.optimization_barrier((block, earlier))[0]


def hopped(block, hop):
    return lax.ppermute(block, "head", [(i, i ^ hop) for i in range(4)])


def local(
    queries,
    fresh_keyvals,
    ssm_input,
    gate_input,
    state_maps,
    step_logit,
    slot_mask,
    cache_pool,
    page_map,
    cached_lengths,
    prior_state,
    decay_log,
    step_bias,
    skip_gain,
    norm_gain,
):
    rows = ssm_input.shape[0]
    width = MI // 4
    slots, half = cache_pool.shape[0], cache_pool.shape[1]
    far_pool = hopped(cache_pool, 2)
    pages, sent = call(order_kernel, [((slots // 2, 2, half, 2 * HD), BF16)] * 2, [VMEM] * 2)(cache_pool, far_pool)
    told, ahead, far = call(
        pack_kernel,
        [((rows, TOLD), BF16), ((rows, AHEAD), BF16), ((rows, 2 * width + STATE + KEYVALS), BF16)],
        [SMEM] * 3 + [VMEM] * 5,
        limit=60,
    )(
        decay_log, step_bias, skip_gain,
        ssm_input, state_maps, step_logit.T, slot_mask.reshape(1, rows), fresh_keyvals,
    )
    prior1 = hopped(prior_state, 1)
    x1 = hopped(ssm_input, 1)
    kv1 = hopped(fresh_keyvals, 1)
    told1 = hopped(told, 1)
    ahead2 = hopped(ahead, 2)
    far = hopped(far, 2)
    ahead3 = hopped(ahead2, 1)

    parts, bit = [pages], 1
    while bit < slots:
        if bit > 1:
            keep = parts[0].shape[0] // 2
            sent = jnp.concatenate([part[keep:] for part in parts])
            parts = [part[:keep] for part in parts]
        if bit == 2:
            sent = behind(sent, told1)
        came = lax.ppermute(sent, "dp", [(i, i ^ bit) for i in range(slots)])
        keep = parts[0].shape[0]
        parts = parts + [came[i * keep : (i + 1) * keep] for i in range(len(parts))]
        bit *= 2
    y2, shift, total, skip = call(
        remote_kernel,
        [((2 * rows, width), BF16), ((32, 4 * rows), F32), ((4 * rows, LANES), F32), ((8, LANES), F32)],
        [VMEM] * 7,
    )(told, told1, ahead2, ahead3, ssm_input, x1, prior1)
    relayed = hopped(behind(far, y2), 1)
    y2 = hopped(y2, 2)
    (y,) = call(near_kernel, [((rows, MI), F32)], [VMEM] * 11)(
        shift, total, skip, told, told1, ssm_input, x1, far, relayed, prior_state, prior1
    )
    y3 = hopped(behind(y2, y), 1)
    pages = jnp.concatenate(parts)
    pages1 = hopped(pages, 1)
    (attended,) = call(attention_kernel, [((rows, QH * HD), BF16)], [SMEM] * 2 + [VMEM] * 11)(
        page_map, cached_lengths, queries, pages, pages1,
        fresh_keyvals, kv1, far, relayed, told, told1, ahead2, ahead3,
    )
    (result,) = call(
        final_kernel,
        [((rows, QH * HD + MI), BF16)],
        [VMEM] * 6,
        [pltpu.VMEM((rows, MI), F32)],
    )(attended, gate_input, norm_gain.reshape(1, MI), y, y2, y3)
    return result


def solution(mesh):
    in_specs = (
        P(("dp", "head"), None),
        P(("dp", "head"), None),
        P(("dp", "head"), None),
        P(("dp", "head"), None),
        P(("dp", "head"), None),
        P(("dp", "head"), None),
        P(("dp", "head")),
        P("dp", "head", None),
        P("dp", None),
        P("dp"),
        P("dp", "head", None, None),
        P("head"),
        P("head"),
        P("head"),
        P(),
    )
    out_specs = P(("dp", "head"), None)
    return jax.shard_map(local, mesh=mesh, in_specs=in_specs, out_specs=out_specs, check_vma=False)
```

```python
import math

import jax
import jax.numpy as jnp
from jax import lax
from jax.experimental import pallas as pl
from jax.experimental.pallas import tpu as pltpu
from jax.sharding import PartitionSpec as P

HD = 128
QH = 12
KVH = 2
GROUP = QH // KVH
STATE = 256
MI = 3072
PAGE = 16
LANES = 128
EPSILON = 1e-05
BF16 = jnp.bfloat16
F32 = jnp.float32
HIGHEST = lax.Precision.HIGHEST
VMEM = pl.BlockSpec(memory_space=pltpu.VMEM)
SMEM = pl.BlockSpec(memory_space=pltpu.SMEM)
ANY = pl.BlockSpec(memory_space=pl.ANY)
NOTES = slice(STATE, STATE + LANES)
AHEAD = STATE + LANES
IN_MAP = slice(AHEAD, AHEAD + STATE)
TOLD = AHEAD + STATE
KEYVALS = 2 * KVH * HD
MASK_LANE = 24
PARAM_LANE = 32
ALL_HEADS = 24


def call(kernel, outs, specs, scratch=(), limit=24):
    return pl.pallas_call(
        kernel,
        out_shape=[jax.ShapeDtypeStruct(shape, dtype) for shape, dtype in outs],
        in_specs=specs,
        out_specs=[VMEM] * len(outs),
        scratch_shapes=list(scratch),
        compiler_params=pltpu.CompilerParams(vmem_limit_bytes=limit << 20),
    )


def columns(ref, owner, width):
    return ref[:, pl.ds(pl.multiple_of(owner * width, LANES), width)]


def iota(shape, dim):
    return lax.broadcasted_iota(jnp.int32, shape, dim)


def rolled(array, first, axis):
    size = array.shape[axis]
    return pltpu.roll(array, lax.rem(size - first, size), axis)


def nt_dot(a, b, precision=None):
    return lax.dot_general(
        a, b, (((1,), (1,)), ((), ())), preferred_element_type=F32, precision=precision
    )


def pack_kernel(
    log_rate_ref, bias_ref, skip_ref, x_ref, maps_ref, logit_ref, mask_ref, keyval_ref, told_ref, ahead_ref, far_ref,
):
    me = lax.axis_index("head")
    rows, width = x_ref.shape[0], x_ref.shape[1] // 4
    far_ref[:, :width] = columns(x_ref, me ^ 2, width)
    far_ref[:, width : 2 * width] = columns(x_ref, me ^ 3, width)
    far_ref[:, 2 * width : 2 * width + STATE] = maps_ref[:, :STATE]
    far_ref[:, 2 * width + STATE :] = keyval_ref[...]
    told_ref[:, IN_MAP] = maps_ref[:, :STATE]
    told_ref[:, :STATE] = maps_ref[:, STATE:]
    ahead_ref[:, :STATE] = maps_ref[:, STATE:]
    heads, head_count = logit_ref.shape[0], log_rate_ref.shape[0]
    pick = (iota((heads, LANES), 0) == iota((heads, LANES), 1)).astype(F32).astype(BF16)
    notes = lax.dot_general(logit_ref[...], pick, (((0,), (0,)), ((), ())), preferred_element_type=F32)
    diagonal = iota((rows, rows), 0) == iota((rows, rows), 1)
    real = jnp.broadcast_to(mask_ref[...], (rows, rows)) > 0
    real = jnp.sum(jnp.where(diagonal & real, 1.0, 0.0), axis=1, keepdims=True)
    lane, row = iota((1, LANES), 1), iota((rows, 1), 0)
    params = jnp.zeros((rows, LANES), F32)
    for kind, ref in enumerate((log_rate_ref, bias_ref, skip_ref)):
        value = jnp.zeros((1, LANES), F32)
        for head in range(head_count):
            value = jnp.where(lane == PARAM_LANE + me * head_count + head, ref[head], value)
        high = value.astype(BF16).astype(F32)
        middle = (value - high).astype(BF16).astype(F32)
        for part, piece in enumerate((high, middle, value - high - middle)):
            params = jnp.where(row == 3 * kind + part, piece, params)
    in_params = (lane >= PARAM_LANE) & (lane < PARAM_LANE + ALL_HEADS)
    notes = jnp.where(lane < heads, notes, jnp.where(in_params, params, real))
    told_ref[:, NOTES] = notes.astype(BF16)
    ahead_ref[:, NOTES] = notes.astype(BF16)


def order_kernel(pool_ref, far_pool_ref, even_ref, odd_ref):
    request = lax.axis_index("dp")
    half_slots = even_ref.shape[0]

    def place(at, carry):
        distance, rest, bit = 0, at, half_slots
        while bit > 1:
            distance, rest, bit = distance + (rest % 2) * bit, rest // 2, bit // 2
        for chip, ref in enumerate((pool_ref, far_pool_ref)):
            even_ref[at, chip] = ref[request ^ distance]
            odd_ref[at, chip] = ref[request ^ distance ^ 1]
        return carry

    lax.fori_loop(0, half_slots, place, 0, unroll=half_slots <= 8)


def token_at(index, rows, me):
    return (me ^ (index // rows)) * rows + index % rows


def head_sums(tolds, me):
    rows = tolds[0].shape[0]
    span = 4 * rows
    notes = jnp.concatenate([ref[:, NOTES] for ref in tolds], axis=0)
    params = sum(ref[0:16, NOTES].astype(F32) for ref in tolds).astype(BF16)
    head, lane = iota((32, LANES), 0), iota((32, LANES), 1)
    by_row = jnp.where(head == lane, 1.0, 0.0).astype(BF16)
    by_row_params = jnp.where(head + PARAM_LANE == lane, 1.0, 0.0).astype(BF16)
    row_params = nt_dot(by_row_params, params)
    source, target = iota((LANES, LANES), 0), iota((LANES, LANES), 1)
    by_lane_params = jnp.where((source == target + PARAM_LANE) & (target < ALL_HEADS), 1.0, 0.0).astype(BF16)
    skips = jnp.dot(params, by_lane_params, preferred_element_type=F32)
    skip = skips[6:7, :] + skips[7:8, :] + skips[8:9, :]

    def row_param(kind):
        return sum(row_params[:, 3 * kind + part : 3 * kind + part + 1] for part in range(3))

    logits = nt_dot(by_row, notes)
    steps = jnp.log(1.0 + jnp.exp(logits + row_param(1))) * logits[MASK_LANE : MASK_LANE + 1, :]
    token = token_at(iota((span, span), 0), rows, me)
    source = token_at(iota((span, span), 1), rows, me)
    upto = jnp.where(source <= token, 1.0, 0.0)
    sums = nt_dot(-jnp.exp(row_param(0)) * steps, upto, HIGHEST)
    by_token = jnp.concatenate([sums] * (LANES // 32), axis=0).T
    return sums - jnp.log(steps), by_token, skip


def remote_kernel(
    told0, told1, ahead2, ahead3, x0_ref, x1_ref, prior1_ref,
    y_ref, shift_ref, total_ref, skip_ref,
):
    me = lax.axis_index("head")
    rows, width = told0.shape[0], y_ref.shape[1]
    near, head_count = 2 * rows, width // HD
    shift, total, skip = head_sums((told0, told1, ahead2, ahead3), me)
    shift_ref[...] = shift
    total_ref[...] = total
    skip_ref[...] = jnp.broadcast_to(skip, skip_ref.shape)
    block = me ^ 1
    block_shift = rolled(shift, block * head_count, 0)
    block_total = rolled(total[near:], block * head_count, 1)
    mask = jnp.concatenate([ref[:, STATE + MASK_LANE : STATE + MASK_LANE + 1] for ref in (ahead2, ahead3)], axis=0)
    mask = mask.astype(F32)
    out_map = jnp.concatenate([ahead2[:, :STATE], ahead3[:, :STATE]], axis=0)
    from_prior = nt_dot(out_map, prior1_ref[0].reshape(width, STATE))

    def write(from_x):
        for head in range(head_count):
            cols = slice(head * HD, (head + 1) * HD)
            sums = block_total[:, head : head + 1]
            y = from_prior[:, cols] * jnp.exp(sums)
            if from_x is not None:
                y = y + from_x(cols, sums - block_shift[head : head + 1, :near])
            y_ref[:, cols] = (y * mask).astype(BF16)

    @pl.when(me < 2)
    def _():
        in_map = jnp.concatenate([told0[:, IN_MAP], told1[:, IN_MAP]], axis=0)
        products = nt_dot(out_map, in_map)
        x = jnp.concatenate([columns(x0_ref, block, width), columns(x1_ref, block, width)], axis=0)

        def from_x(cols, gaps):
            return jnp.dot((jnp.exp(gaps) * products).astype(BF16), x[:, cols], preferred_element_type=F32)

        write(from_x)

    @pl.when(me >= 2)
    def _():
        write(None)


def near_kernel(
    shift_ref, total_ref, skip_ref, told0, told1, x0_ref, x1_ref, far_ref, relayed_ref,
    prior0_ref, prior1_ref, y_ref,
):
    me = lax.axis_index("head")
    rows, width = told0.shape[0], x0_ref.shape[1] // 4
    near, span, head_count = 2 * rows, 4 * rows, width // HD
    far_map = slice(2 * width, 2 * width + STATE)
    out_map = told0[:, :STATE]
    mask = told0[:, STATE + MASK_LANE : STATE + MASK_LANE + 1].astype(F32)
    shift, total, skip = shift_ref[...], total_ref[:rows, :], skip_ref[...]

    def write(with_far):
        whole = span if with_far else near
        in_map = [told0[:, IN_MAP], told1[:, IN_MAP]]
        if with_far:
            in_map += [far_ref[:, far_map], relayed_ref[:, far_map]]
        products = nt_dot(out_map, jnp.concatenate(in_map, axis=0))
        token = token_at(iota((rows, whole), 0), rows, me)
        source = token_at(iota((rows, whole), 1), rows, me)
        causal = jnp.where(source <= token, 0.0, -jnp.inf)
        for hop in range(4):
            block = me ^ hop
            block_shift = rolled(shift, block * head_count, 0)
            block_total = rolled(total, block * head_count, 1)
            block_skip = rolled(skip, block * head_count, 1)[0:1, :]
            own = columns(x0_ref, block, width)
            sources = [own, columns(x1_ref, block, width)]
            reach = near
            if hop < 2:
                reach = whole
                from_prior = nt_dot(out_map, (prior0_ref, prior1_ref)[hop][0].reshape(width, STATE))
            if reach == span:
                place = (hop, 1 - hop)
                sources += [ref[:, at * width : (at + 1) * width] for ref, at in zip((far_ref, relayed_ref), place)]
            sources = jnp.concatenate(sources, axis=0)
            for head in range(head_count):
                cols = slice(head * HD, (head + 1) * HD)
                sums = block_total[:, head : head + 1]
                weights = jnp.exp(sums - block_shift[head : head + 1, :reach] + causal[:, :reach]) * products[:, :reach]
                y = jnp.dot(weights.astype(BF16), sources[:, cols], preferred_element_type=F32)
                y = y + block_skip[:, head : head + 1] * own[:, cols].astype(F32)
                if hop < 2:
                    y = y + from_prior[:, cols] * jnp.exp(sums)
                y_ref[:, hop * width + head * HD : hop * width + (head + 1) * HD] = y * mask

    @pl.when(me < 2)
    def _():
        write(False)

    @pl.when(me >= 2)
    def _():
        write(True)


def attention_kernel(
    page_map_ref, length_ref, query_ref, pages0, pages1,
    kv0, kv1, far_ref, relayed_ref, told0, told1, told2, told3, out_ref,
):
    me = lax.axis_index("head")
    request = lax.axis_index("dp")
    rows = query_ref.shape[0]
    slots, half = pages0.shape[0], pages0.shape[2]
    part = slots * half
    cached = 2 * part
    inv_scale = 1.0 / math.sqrt(HD)
    square, wide = (slots, slots), (slots, cached)
    holders = jnp.where(iota(square, 0) == iota(square, 1), jnp.broadcast_to(page_map_ref[...], square), 0)
    holders = jnp.sum(holders.astype(F32), axis=1, keepdims=True).astype(jnp.int32)
    page = jnp.where((holders ^ request) == iota(wide, 1) % part // half, iota(wide, 0), 0)
    page = jnp.sum(page.astype(F32), axis=0, keepdims=True).astype(jnp.int32)
    lane = iota((1, cached), 1)
    position = page * PAGE + ((me ^ (lane // part)) % 2) * half + lane % half
    old_shut = jnp.broadcast_to(jnp.where(position < length_ref[...], 0.0, -jnp.inf), (rows, cached))
    ones = jnp.where(iota((8, LANES), 1) == MASK_LANE, 1.0, 0.0).astype(BF16)
    token, source = iota((rows, rows), 0), iota((rows, rows), 1)
    keep = told0[:, STATE + MASK_LANE : STATE + MASK_LANE + 1].astype(F32)
    pages = [ref[:, chip].reshape(part, 2 * HD) for chip in range(2) for ref in (pages0, pages1)]

    def write(reach):
        shut = [old_shut]
        for hop, ref in enumerate((told0, told1, told2, told3)[:reach]):
            real = nt_dot(ones, ref[:, NOTES])[0:1, :] > 0.5
            limit = token if hop == 0 else jnp.where((me ^ hop) < me, rows, -1)
            shut.append(jnp.where(real & (source <= limit), 0.0, -jnp.inf))
        shut = jnp.concatenate(shut, axis=1)
        shut = jnp.concatenate([shut] * GROUP, axis=0)
        for group in range(KVH):
            queries = jnp.concatenate(
                [query_ref[:, (group * GROUP + h) * HD : (group * GROUP + h + 1) * HD] for h in range(GROUP)],
                axis=0,
            )
            here = jnp.broadcast_to(me // 2, (part, 2 * HD)) == group
            every = [jnp.where(here, pages[core], pages[core ^ 2]) for core in range(2)]
            for ref in (kv0, kv1, far_ref, relayed_ref)[:reach]:
                start = ref.shape[1] - KEYVALS + 2 * group * HD
                every.append(ref[:, start : start + 2 * HD])
            every = jnp.concatenate(every, axis=0)
            keys, values = every[:, :HD], every[:, HD:]
            scores = nt_dot(queries, keys) * inv_scale + shut
            top = jnp.max(scores, axis=1, keepdims=True)
            terms = jnp.exp(scores - top)
            total = jnp.sum(terms, axis=1, keepdims=True)
            mixed = jnp.dot(terms.astype(BF16), values, preferred_element_type=F32) / total
            for h in range(GROUP):
                head = group * GROUP + h
                out_ref[:, head * HD : (head + 1) * HD] = (mixed[h * rows : (h + 1) * rows] * keep).astype(BF16)

    @pl.when(me < 2)
    def _():
        write(2)

    @pl.when(me >= 2)
    def _():
        write(4)


def final_kernel(attended_ref, gate_ref, gain_ref, y_ref, y2_ref, y3_ref, out_ref, gated):
    me = lax.axis_index("head")
    rows, width = y_ref.shape[0], y2_ref.shape[1]
    heads_width = attended_ref.shape[1]
    out_ref[:, :heads_width] = attended_ref[...]
    squares = jnp.zeros((rows, 1), F32)
    for hop, far in enumerate((None, None, y3_ref[rows:, :], y2_ref[:rows, :])):
        gate = columns(gate_ref, me ^ hop, width).astype(F32)
        part = y_ref[:, hop * width : (hop + 1) * width]
        if far is not None:
            part = part + far.astype(F32)
        part = part.astype(BF16).astype(F32) * (gate / (1.0 + jnp.exp(-gate)))
        gated[:, hop * width : (hop + 1) * width] = part
        squares = squares + jnp.sum(part * part, axis=1, keepdims=True)
    scale = lax.rsqrt(squares / MI + EPSILON)
    for hop in range(4):
        gain = columns(gain_ref, me ^ hop, width)
        part = gated[:, hop * width : (hop + 1) * width] * scale * gain
        start = pl.multiple_of(heads_width + (me ^ hop) * width, LANES)
        out_ref[:, pl.ds(start, width)] = part.astype(BF16)


def behind(block, earlier):
    return lax.optimization_barrier((block, earlier))[0]


def hopped(block, hop):
    return lax.ppermute(block, "head", [(i, i ^ hop) for i in range(4)])


def local(
    queries,
    fresh_keyvals,
    ssm_input,
    gate_input,
    state_maps,
    step_logit,
    slot_mask,
    cache_pool,
    page_map,
    cached_lengths,
    prior_state,
    decay_log,
    step_bias,
    skip_gain,
    norm_gain,
):
    rows = ssm_input.shape[0]
    width = MI // 4
    slots, half = cache_pool.shape[0], cache_pool.shape[1]
    far_pool = hopped(cache_pool, 2)
    pages, sent = call(order_kernel, [((slots // 2, 2, half, 2 * HD), BF16)] * 2, [VMEM] * 2)(cache_pool, far_pool)
    told, ahead, far = call(
        pack_kernel,
        [((rows, TOLD), BF16), ((rows, AHEAD), BF16), ((rows, 2 * width + STATE + KEYVALS), BF16)],
        [SMEM] * 3 + [VMEM] * 5,
        limit=60,
    )(
        decay_log, step_bias, skip_gain,
        ssm_input, state_maps, step_logit.T, slot_mask.reshape(1, rows), fresh_keyvals,
    )
    prior1 = hopped(prior_state, 1)
    x1 = hopped(ssm_input, 1)
    kv1 = hopped(fresh_keyvals, 1)
    told1 = hopped(told, 1)
    ahead2 = hopped(ahead, 2)
    far = hopped(far, 2)
    ahead3 = hopped(ahead2, 1)

    parts, bit = [pages], 1
    while bit < slots:
        if bit > 1:
            keep = parts[0].shape[0] // 2
            sent = jnp.concatenate([part[keep:] for part in parts])
            parts = [part[:keep] for part in parts]
        if bit == 2:
            sent = behind(sent, told1)
        came = lax.ppermute(sent, "dp", [(i, i ^ bit) for i in range(slots)])
        keep = parts[0].shape[0]
        parts = parts + [came[i * keep : (i + 1) * keep] for i in range(len(parts))]
        bit *= 2
    y2, shift, total, skip = call(
        remote_kernel,
        [((2 * rows, width), BF16), ((32, 4 * rows), F32), ((4 * rows, LANES), F32), ((8, LANES), F32)],
        [VMEM] * 7,
    )(told, told1, ahead2, ahead3, ssm_input, x1, prior1)
    relayed = hopped(behind(far, y2), 1)
    y2 = hopped(y2, 2)
    (y,) = call(near_kernel, [((rows, MI), F32)], [VMEM] * 11)(
        shift, total, skip, told, told1, ssm_input, x1, far, relayed, prior_state, prior1
    )
    y3 = hopped(behind(y2, y), 1)
    pages = jnp.concatenate(parts)
    pages1 = hopped(pages, 1)
    (attended,) = call(attention_kernel, [((rows, QH * HD), BF16)], [VMEM] * 13)(
        page_map, cached_lengths.reshape(1, 1), queries, pages, pages1,
        fresh_keyvals, kv1, far, relayed, told, told1, ahead2, ahead3,
    )
    (result,) = call(
        final_kernel,
        [((rows, QH * HD + MI), BF16)],
        [VMEM] * 6,
        [pltpu.VMEM((rows, MI), F32)],
    )(attended, gate_input, norm_gain.reshape(1, MI), y, y2, y3)
    return result


def solution(mesh):
    in_specs = (
        P(("dp", "head"), None),
        P(("dp", "head"), None),
        P(("dp", "head"), None),
        P(("dp", "head"), None),
        P(("dp", "head"), None),
        P(("dp", "head"), None),
        P(("dp", "head")),
        P("dp", "head", None),
        P("dp", None),
        P("dp"),
        P("dp", "head", None, None),
        P("head"),
        P("head"),
        P("head"),
        P(),
    )
    out_specs = P(("dp", "head"), None)
    return jax.shard_map(local, mesh=mesh, in_specs=in_specs, out_specs=out_specs, check_vma=False)
```

```python
import math

import jax
import jax.numpy as jnp
from jax import lax
from jax.experimental import pallas as pl
from jax.experimental.pallas import tpu as pltpu
from jax.sharding import PartitionSpec as P

HD = 128
QH = 12
KVH = 2
GROUP = QH // KVH
STATE = 256
MI = 3072
PAGE = 16
LANES = 128
EPSILON = 1e-05
SCAN_COST = 3 * 10**8
ATTEND_COST = 10**9
PACK_COST = 3 * 10**9
ORDER_COST = 3 * 10**8
BF16 = jnp.bfloat16
F32 = jnp.float32
HIGHEST = lax.Precision.HIGHEST
VMEM = pl.BlockSpec(memory_space=pltpu.VMEM)
SMEM = pl.BlockSpec(memory_space=pltpu.SMEM)
NOTES = slice(STATE, STATE + LANES)
AHEAD = STATE + LANES
IN_MAP = slice(AHEAD, AHEAD + STATE)
TOLD = AHEAD + STATE
KEYVALS = 2 * KVH * HD
MASK_LANE = 24
PARAM_LANE = 32
ALL_HEADS = 24


def call(kernel, outs, specs, scratch=(), limit=24, flops=0):
    cost = pl.CostEstimate(flops=flops, bytes_accessed=0, transcendentals=0) if flops else None
    return pl.pallas_call(
        kernel,
        cost_estimate=cost,
        out_shape=[jax.ShapeDtypeStruct(shape, dtype) for shape, dtype in outs],
        in_specs=specs,
        out_specs=[VMEM] * len(outs),
        scratch_shapes=list(scratch),
        compiler_params=pltpu.CompilerParams(vmem_limit_bytes=limit << 20),
    )


def columns(ref, owner, width):
    return ref[:, pl.ds(pl.multiple_of(owner * width, LANES), width)]


def iota(shape, dim):
    return lax.broadcasted_iota(jnp.int32, shape, dim)


def rolled(array, first, axis):
    size = array.shape[axis]
    return pltpu.roll(array, lax.rem(size - first, size), axis)


def nt_dot(a, b, precision=None):
    return lax.dot_general(
        a, b, (((1,), (1,)), ((), ())), preferred_element_type=F32, precision=precision
    )


def pack_kernel(
    log_rate_ref, bias_ref, skip_ref, x_ref, maps_ref, logit_ref, mask_ref, keyval_ref, told_ref, ahead_ref, far_ref,
):
    me = lax.axis_index("head")
    rows, width = x_ref.shape[0], x_ref.shape[1] // 4
    far_ref[:, :width] = columns(x_ref, me ^ 2, width)
    far_ref[:, width : 2 * width] = columns(x_ref, me ^ 3, width)
    far_ref[:, 2 * width : 2 * width + STATE] = maps_ref[:, :STATE]
    far_ref[:, 2 * width + STATE :] = keyval_ref[...]
    told_ref[:, IN_MAP] = maps_ref[:, :STATE]
    told_ref[:, :STATE] = maps_ref[:, STATE:]
    ahead_ref[:, :STATE] = maps_ref[:, STATE:]
    heads, head_count = logit_ref.shape[0], log_rate_ref.shape[0]
    pick = (iota((heads, LANES), 0) == iota((heads, LANES), 1)).astype(F32).astype(BF16)
    notes = lax.dot_general(logit_ref[...], pick, (((0,), (0,)), ((), ())), preferred_element_type=F32)
    diagonal = iota((rows, rows), 0) == iota((rows, rows), 1)
    real = jnp.broadcast_to(mask_ref[...], (rows, rows)) > 0
    real = jnp.sum(jnp.where(diagonal & real, 1.0, 0.0), axis=1, keepdims=True)
    lane, row = iota((1, LANES), 1), iota((rows, 1), 0)
    params = jnp.zeros((rows, LANES), F32)
    for kind, ref in enumerate((log_rate_ref, bias_ref, skip_ref)):
        value = jnp.zeros((1, LANES), F32)
        for head in range(head_count):
            value = jnp.where(lane == PARAM_LANE + me * head_count + head, ref[head], value)
        high = value.astype(BF16).astype(F32)
        middle = (value - high).astype(BF16).astype(F32)
        for part, piece in enumerate((high, middle, value - high - middle)):
            params = jnp.where(row == 3 * kind + part, piece, params)
    in_params = (lane >= PARAM_LANE) & (lane < PARAM_LANE + ALL_HEADS)
    notes = jnp.where(lane < heads, notes, jnp.where(in_params, params, real))
    told_ref[:, NOTES] = notes.astype(BF16)
    ahead_ref[:, NOTES] = notes.astype(BF16)


def order_kernel(pool_ref, far_pool_ref, even_ref, odd_ref):
    request = lax.axis_index("dp")
    half_slots = even_ref.shape[0]

    def place(at, carry):
        distance, rest, bit = 0, at, half_slots
        while bit > 1:
            distance, rest, bit = distance + (rest % 2) * bit, rest // 2, bit // 2
        for chip, ref in enumerate((pool_ref, far_pool_ref)):
            even_ref[at, chip] = ref[request ^ distance]
            odd_ref[at, chip] = ref[request ^ distance ^ 1]
        return carry

    lax.fori_loop(0, half_slots, place, 0, unroll=half_slots <= 8)


def token_at(index, rows, me):
    return (me ^ (index // rows)) * rows + index % rows


def head_sums(tolds, me):
    rows = tolds[0].shape[0]
    span = 4 * rows
    notes = jnp.concatenate([ref[:, NOTES] for ref in tolds], axis=0)
    params = sum(ref[0:16, NOTES].astype(F32) for ref in tolds).astype(BF16)
    head, lane = iota((32, LANES), 0), iota((32, LANES), 1)
    by_row = jnp.where(head == lane, 1.0, 0.0).astype(BF16)
    by_row_params = jnp.where(head + PARAM_LANE == lane, 1.0, 0.0).astype(BF16)
    row_params = nt_dot(by_row_params, params)
    source, target = iota((LANES, LANES), 0), iota((LANES, LANES), 1)
    by_lane_params = jnp.where((source == target + PARAM_LANE) & (target < ALL_HEADS), 1.0, 0.0).astype(BF16)
    skips = jnp.dot(params, by_lane_params, preferred_element_type=F32)
    skip = skips[6:7, :] + skips[7:8, :] + skips[8:9, :]

    def row_param(kind):
        return sum(row_params[:, 3 * kind + part : 3 * kind + part + 1] for part in range(3))

    logits = nt_dot(by_row, notes)
    steps = jnp.log(1.0 + jnp.exp(logits + row_param(1))) * logits[MASK_LANE : MASK_LANE + 1, :]
    token = token_at(iota((span, span), 0), rows, me)
    source = token_at(iota((span, span), 1), rows, me)
    upto = jnp.where(source <= token, 1.0, 0.0)
    sums = nt_dot(-jnp.exp(row_param(0)) * steps, upto, HIGHEST)
    by_token = jnp.concatenate([sums] * (LANES // 32), axis=0).T
    return sums - jnp.log(steps), by_token, skip


def remote_kernel(
    told0, told1, ahead2, ahead3, x0_ref, x1_ref, prior1_ref,
    y_ref, shift_ref, total_ref, skip_ref,
):
    me = lax.axis_index("head")
    rows, width = told0.shape[0], y_ref.shape[1]
    near, head_count = 2 * rows, width // HD
    shift, total, skip = head_sums((told0, told1, ahead2, ahead3), me)
    shift_ref[...] = shift
    total_ref[...] = total
    skip_ref[...] = jnp.broadcast_to(skip, skip_ref.shape)
    block = me ^ 1
    block_shift = rolled(shift, block * head_count, 0)
    block_total = rolled(total[near:], block * head_count, 1)
    mask = jnp.concatenate([ref[:, STATE + MASK_LANE : STATE + MASK_LANE + 1] for ref in (ahead2, ahead3)], axis=0)
    mask = mask.astype(F32)
    out_map = jnp.concatenate([ahead2[:, :STATE], ahead3[:, :STATE]], axis=0)
    from_prior = nt_dot(out_map, prior1_ref[0].reshape(width, STATE))

    def write(from_x):
        for head in range(head_count):
            cols = slice(head * HD, (head + 1) * HD)
            sums = block_total[:, head : head + 1]
            y = from_prior[:, cols] * jnp.exp(sums)
            if from_x is not None:
                y = y + from_x(cols, sums - block_shift[head : head + 1, :near])
            y_ref[:, cols] = (y * mask).astype(BF16)

    @pl.when(me < 2)
    def _():
        in_map = jnp.concatenate([told0[:, IN_MAP], told1[:, IN_MAP]], axis=0)
        products = nt_dot(out_map, in_map)
        x = jnp.concatenate([columns(x0_ref, block, width), columns(x1_ref, block, width)], axis=0)

        def from_x(cols, gaps):
            return jnp.dot((jnp.exp(gaps) * products).astype(BF16), x[:, cols], preferred_element_type=F32)

        write(from_x)

    @pl.when(me >= 2)
    def _():
        write(None)


def near_kernel(
    shift_ref, total_ref, skip_ref, told0, told1, x0_ref, x1_ref, far_ref, relayed_ref,
    prior0_ref, prior1_ref, y_ref,
):
    me = lax.axis_index("head")
    rows, width = told0.shape[0], x0_ref.shape[1] // 4
    near, span, head_count = 2 * rows, 4 * rows, width // HD
    far_map = slice(2 * width, 2 * width + STATE)
    out_map = told0[:, :STATE]
    mask = told0[:, STATE + MASK_LANE : STATE + MASK_LANE + 1].astype(F32)
    shift, total, skip = shift_ref[...], total_ref[:rows, :], skip_ref[...]

    def write(with_far):
        whole = span if with_far else near
        in_map = [told0[:, IN_MAP], told1[:, IN_MAP]]
        if with_far:
            in_map += [far_ref[:, far_map], relayed_ref[:, far_map]]
        products = nt_dot(out_map, jnp.concatenate(in_map, axis=0))
        token = token_at(iota((rows, whole), 0), rows, me)
        source = token_at(iota((rows, whole), 1), rows, me)
        causal = jnp.where(source <= token, 0.0, -jnp.inf)
        for hop in range(4):
            block = me ^ hop
            block_shift = rolled(shift, block * head_count, 0)
            block_total = rolled(total, block * head_count, 1)
            block_skip = rolled(skip, block * head_count, 1)[0:1, :]
            own = columns(x0_ref, block, width)
            sources = [own, columns(x1_ref, block, width)]
            reach = near
            if hop < 2:
                reach = whole
                from_prior = nt_dot(out_map, (prior0_ref, prior1_ref)[hop][0].reshape(width, STATE))
            if reach == span:
                place = (hop, 1 - hop)
                sources += [ref[:, at * width : (at + 1) * width] for ref, at in zip((far_ref, relayed_ref), place)]
            sources = jnp.concatenate(sources, axis=0)
            for head in range(head_count):
                cols = slice(head * HD, (head + 1) * HD)
                sums = block_total[:, head : head + 1]
                weights = jnp.exp(sums - block_shift[head : head + 1, :reach] + causal[:, :reach]) * products[:, :reach]
                y = jnp.dot(weights.astype(BF16), sources[:, cols], preferred_element_type=F32)
                y = y + block_skip[:, head : head + 1] * own[:, cols].astype(F32)
                if hop < 2:
                    y = y + from_prior[:, cols] * jnp.exp(sums)
                y_ref[:, hop * width + head * HD : hop * width + (head + 1) * HD] = y * mask

    @pl.when(me < 2)
    def _():
        write(False)

    @pl.when(me >= 2)
    def _():
        write(True)


def attention_kernel(
    page_map_ref, length_ref, query_ref, pages0, pages1,
    kv0, kv1, far_ref, relayed_ref, told0, told1, told2, told3, out_ref,
):
    me = lax.axis_index("head")
    request = lax.axis_index("dp")
    rows = query_ref.shape[0]
    slots, half = pages0.shape[0], pages0.shape[2]
    part = slots * half
    cached = 2 * part
    inv_scale = 1.0 / math.sqrt(HD)
    square, wide = (slots, slots), (slots, cached)
    holders = jnp.where(iota(square, 0) == iota(square, 1), jnp.broadcast_to(page_map_ref[...], square), 0)
    holders = jnp.sum(holders.astype(F32), axis=1, keepdims=True).astype(jnp.int32)
    page = jnp.where((holders ^ request) == iota(wide, 1) % part // half, iota(wide, 0), 0)
    page = jnp.sum(page.astype(F32), axis=0, keepdims=True).astype(jnp.int32)
    lane = iota((1, cached), 1)
    position = page * PAGE + ((me ^ (lane // part)) % 2) * half + lane % half
    old_shut = jnp.broadcast_to(jnp.where(position < length_ref[...], 0.0, -jnp.inf), (rows, cached))
    ones = jnp.where(iota((8, LANES), 1) == MASK_LANE, 1.0, 0.0).astype(BF16)
    token, source = iota((rows, rows), 0), iota((rows, rows), 1)
    keep = told0[:, STATE + MASK_LANE : STATE + MASK_LANE + 1].astype(F32)
    pages = [ref[:, chip].reshape(part, 2 * HD) for chip in range(2) for ref in (pages0, pages1)]

    def write(reach):
        shut = [old_shut]
        for hop, ref in enumerate((told0, told1, told2, told3)[:reach]):
            real = nt_dot(ones, ref[:, NOTES])[0:1, :] > 0.5
            limit = token if hop == 0 else jnp.where((me ^ hop) < me, rows, -1)
            shut.append(jnp.where(real & (source <= limit), 0.0, -jnp.inf))
        shut = jnp.concatenate(shut, axis=1)
        shut = jnp.concatenate([shut] * GROUP, axis=0)
        for group in range(KVH):
            queries = jnp.concatenate(
                [query_ref[:, (group * GROUP + h) * HD : (group * GROUP + h + 1) * HD] for h in range(GROUP)],
                axis=0,
            )
            here = jnp.broadcast_to(me // 2, (part, 2 * HD)) == group
            every = [jnp.where(here, pages[core], pages[core ^ 2]) for core in range(2)]
            for ref in (kv0, kv1, far_ref, relayed_ref)[:reach]:
                start = ref.shape[1] - KEYVALS + 2 * group * HD
                every.append(ref[:, start : start + 2 * HD])
            every = jnp.concatenate(every, axis=0)
            keys, values = every[:, :HD], every[:, HD:]
            scores = nt_dot(queries, keys) * inv_scale + shut
            top = jnp.max(scores, axis=1, keepdims=True)
            terms = jnp.exp(scores - top)
            total = jnp.sum(terms, axis=1, keepdims=True)
            mixed = jnp.dot(terms.astype(BF16), values, preferred_element_type=F32) / total
            for h in range(GROUP):
                head = group * GROUP + h
                out_ref[:, head * HD : (head + 1) * HD] = (mixed[h * rows : (h + 1) * rows] * keep).astype(BF16)

    @pl.when(me < 2)
    def _():
        write(2)

    @pl.when(me >= 2)
    def _():
        write(4)


def final_kernel(attended_ref, gate_ref, gain_ref, y_ref, y2_ref, y3_ref, out_ref, gated):
    me = lax.axis_index("head")
    rows, width = y_ref.shape[0], y2_ref.shape[1]
    heads_width = attended_ref.shape[1]
    out_ref[:, :heads_width] = attended_ref[...]
    squares = jnp.zeros((rows, 1), F32)
    for hop, far in enumerate((None, None, y3_ref[rows:, :], y2_ref[:rows, :])):
        gate = columns(gate_ref, me ^ hop, width).astype(F32)
        part = y_ref[:, hop * width : (hop + 1) * width]
        if far is not None:
            part = part + far.astype(F32)
        part = part.astype(BF16).astype(F32) * (gate / (1.0 + jnp.exp(-gate)))
        gated[:, hop * width : (hop + 1) * width] = part
        squares = squares + jnp.sum(part * part, axis=1, keepdims=True)
    scale = lax.rsqrt(squares / MI + EPSILON)
    for hop in range(4):
        gain = columns(gain_ref, me ^ hop, width)
        part = gated[:, hop * width : (hop + 1) * width] * scale * gain
        start = pl.multiple_of(heads_width + (me ^ hop) * width, LANES)
        out_ref[:, pl.ds(start, width)] = part.astype(BF16)


def behind(block, earlier):
    return lax.optimization_barrier((block, earlier))[0]


def hopped(block, hop):
    return lax.ppermute(block, "head", [(i, i ^ hop) for i in range(4)])


def local(
    queries,
    fresh_keyvals,
    ssm_input,
    gate_input,
    state_maps,
    step_logit,
    slot_mask,
    cache_pool,
    page_map,
    cached_lengths,
    prior_state,
    decay_log,
    step_bias,
    skip_gain,
    norm_gain,
):
    rows = ssm_input.shape[0]
    width = MI // 4
    slots, half = cache_pool.shape[0], cache_pool.shape[1]
    far_pool = hopped(cache_pool, 2)
    pages, sent = call(order_kernel, [((slots // 2, 2, half, 2 * HD), BF16)] * 2, [VMEM] * 2, flops=ORDER_COST)(cache_pool, far_pool)
    told, ahead, far = call(
        pack_kernel,
        [((rows, TOLD), BF16), ((rows, AHEAD), BF16), ((rows, 2 * width + STATE + KEYVALS), BF16)],
        [SMEM] * 3 + [VMEM] * 5,
        limit=60,
        flops=PACK_COST,
    )(
        decay_log, step_bias, skip_gain,
        ssm_input, state_maps, step_logit.T, slot_mask.reshape(1, rows), fresh_keyvals,
    )
    prior1 = hopped(prior_state, 1)
    x1 = hopped(ssm_input, 1)
    kv1 = hopped(fresh_keyvals, 1)
    told1 = hopped(told, 1)
    ahead2 = hopped(ahead, 2)
    far = hopped(far, 2)
    ahead3 = hopped(ahead2, 1)

    parts, bit = [pages], 1
    while bit < slots:
        if bit > 1:
            keep = parts[0].shape[0] // 2
            sent = jnp.concatenate([part[keep:] for part in parts])
            parts = [part[:keep] for part in parts]
        if bit == 2:
            sent = behind(sent, told1)
        came = lax.ppermute(sent, "dp", [(i, i ^ bit) for i in range(slots)])
        keep = parts[0].shape[0]
        parts = parts + [came[i * keep : (i + 1) * keep] for i in range(len(parts))]
        bit *= 2
    y2, shift, total, skip = call(
        remote_kernel,
        [((2 * rows, width), BF16), ((32, 4 * rows), F32), ((4 * rows, LANES), F32), ((8, LANES), F32)],
        [VMEM] * 7,
        flops=SCAN_COST,
    )(told, told1, ahead2, ahead3, ssm_input, x1, prior1)
    relayed = hopped(behind(far, y2), 1)
    y2 = hopped(y2, 2)
    (y,) = call(near_kernel, [((rows, MI), F32)], [VMEM] * 11)(
        shift, total, skip, told, told1, ssm_input, x1, far, relayed, prior_state, prior1
    )
    y3 = hopped(behind(y2, y), 1)
    pages = jnp.concatenate(parts)
    pages1 = hopped(pages, 1)
    (attended,) = call(attention_kernel, [((rows, QH * HD), BF16)], [VMEM] * 13, flops=ATTEND_COST)(
        page_map, cached_lengths.reshape(1, 1), queries, pages, pages1,
        fresh_keyvals, kv1, far, relayed, told, told1, ahead2, ahead3,
    )
    (result,) = call(
        final_kernel,
        [((rows, QH * HD + MI), BF16)],
        [VMEM] * 6,
        [pltpu.VMEM((rows, MI), F32)],
    )(attended, gate_input, norm_gain.reshape(1, MI), y, y2, y3)
    return result


def solution(mesh):
    in_specs = (
        P(("dp", "head"), None),
        P(("dp", "head"), None),
        P(("dp", "head"), None),
        P(("dp", "head"), None),
        P(("dp", "head"), None),
        P(("dp", "head"), None),
        P(("dp", "head")),
        P("dp", "head", None),
        P("dp", None),
        P("dp"),
        P("dp", "head", None, None),
        P("head"),
        P("head"),
        P("head"),
        P(),
    )
    out_specs = P(("dp", "head"), None)
    return jax.shard_map(local, mesh=mesh, in_specs=in_specs, out_specs=out_specs, check_vma=False)
```

```python
import math

import jax
import jax.numpy as jnp
from jax import lax
from jax.experimental import pallas as pl
from jax.experimental.pallas import tpu as pltpu
from jax.sharding import PartitionSpec as P

HD = 128
QH = 12
KVH = 2
GROUP = QH // KVH
STATE = 256
MI = 3072
PAGE = 16
LANES = 128
EPSILON = 1e-05
SCAN_COST = 3 * 10**8
ATTEND_COST = 10**9
PACK_COST = 3 * 10**9
ORDER_COST = 3 * 10**8
BF16 = jnp.bfloat16
F32 = jnp.float32
HIGHEST = lax.Precision.HIGHEST
VMEM = pl.BlockSpec(memory_space=pltpu.VMEM)
SMEM = pl.BlockSpec(memory_space=pltpu.SMEM)
ANY = pl.BlockSpec(memory_space=pl.ANY)
NOTES = slice(STATE, STATE + LANES)
AHEAD = STATE + LANES
IN_MAP = slice(AHEAD, AHEAD + STATE)
TOLD = AHEAD + STATE
KEYVALS = 2 * KVH * HD
MASK_LANE = 24
PARAM_LANE = 32
ALL_HEADS = 24


def call(kernel, outs, specs, scratch=(), limit=24, flops=0, out_spec=VMEM):
    cost = pl.CostEstimate(flops=flops, bytes_accessed=0, transcendentals=0) if flops else None
    return pl.pallas_call(
        kernel,
        cost_estimate=cost,
        out_shape=[jax.ShapeDtypeStruct(shape, dtype) for shape, dtype in outs],
        in_specs=specs,
        out_specs=[out_spec] * len(outs),
        scratch_shapes=list(scratch),
        compiler_params=pltpu.CompilerParams(vmem_limit_bytes=limit << 20),
    )


def columns(ref, owner, width):
    return ref[:, pl.ds(pl.multiple_of(owner * width, LANES), width)]


def iota(shape, dim):
    return lax.broadcasted_iota(jnp.int32, shape, dim)


def rolled(array, first, axis):
    size = array.shape[axis]
    return pltpu.roll(array, lax.rem(size - first, size), axis)


def nt_dot(a, b, precision=None):
    return lax.dot_general(
        a, b, (((1,), (1,)), ((), ())), preferred_element_type=F32, precision=precision
    )


def pack_kernel(
    log_rate_ref, bias_ref, skip_ref, x_ref, maps_ref, logit_ref, mask_ref, keyval_ref, told_ref, ahead_ref, far_ref,
):
    me = lax.axis_index("head")
    rows, width = x_ref.shape[0], x_ref.shape[1] // 4
    far_ref[:, :width] = columns(x_ref, me ^ 2, width)
    far_ref[:, width : 2 * width] = columns(x_ref, me ^ 3, width)
    far_ref[:, 2 * width : 2 * width + STATE] = maps_ref[:, :STATE]
    far_ref[:, 2 * width + STATE :] = keyval_ref[...]
    told_ref[:, IN_MAP] = maps_ref[:, :STATE]
    told_ref[:, :STATE] = maps_ref[:, STATE:]
    ahead_ref[:, :STATE] = maps_ref[:, STATE:]
    heads, head_count = logit_ref.shape[0], log_rate_ref.shape[0]
    pick = (iota((heads, LANES), 0) == iota((heads, LANES), 1)).astype(F32).astype(BF16)
    notes = lax.dot_general(logit_ref[...], pick, (((0,), (0,)), ((), ())), preferred_element_type=F32)
    diagonal = iota((rows, rows), 0) == iota((rows, rows), 1)
    real = jnp.broadcast_to(mask_ref[...], (rows, rows)) > 0
    real = jnp.sum(jnp.where(diagonal & real, 1.0, 0.0), axis=1, keepdims=True)
    lane, row = iota((1, LANES), 1), iota((rows, 1), 0)
    params = jnp.zeros((rows, LANES), F32)
    for kind, ref in enumerate((log_rate_ref, bias_ref, skip_ref)):
        value = jnp.zeros((1, LANES), F32)
        for head in range(head_count):
            value = jnp.where(lane == PARAM_LANE + me * head_count + head, ref[head], value)
        high = value.astype(BF16).astype(F32)
        middle = (value - high).astype(BF16).astype(F32)
        for part, piece in enumerate((high, middle, value - high - middle)):
            params = jnp.where(row == 3 * kind + part, piece, params)
    in_params = (lane >= PARAM_LANE) & (lane < PARAM_LANE + ALL_HEADS)
    notes = jnp.where(lane < heads, notes, jnp.where(in_params, params, real))
    told_ref[:, NOTES] = notes.astype(BF16)
    ahead_ref[:, NOTES] = notes.astype(BF16)


def order_kernel(pool_ref, far_pool_ref, even_ref, odd_ref):
    request = lax.axis_index("dp")
    half_slots = even_ref.shape[0]

    def place(at, carry):
        distance, rest, bit = 0, at, half_slots
        while bit > 1:
            distance, rest, bit = distance + (rest % 2) * bit, rest // 2, bit // 2
        for chip, ref in enumerate((pool_ref, far_pool_ref)):
            even_ref[at, chip] = ref[request ^ distance]
            odd_ref[at, chip] = ref[request ^ distance ^ 1]
        return carry

    lax.fori_loop(0, half_slots, place, 0, unroll=half_slots <= 8)


def token_at(index, rows, me):
    return (me ^ (index // rows)) * rows + index % rows


def head_sums(tolds, me):
    rows = tolds[0].shape[0]
    span = 4 * rows
    notes = jnp.concatenate([ref[:, NOTES] for ref in tolds], axis=0)
    params = sum(ref[0:16, NOTES].astype(F32) for ref in tolds).astype(BF16)
    head, lane = iota((32, LANES), 0), iota((32, LANES), 1)
    by_row = jnp.where(head == lane, 1.0, 0.0).astype(BF16)
    by_row_params = jnp.where(head + PARAM_LANE == lane, 1.0, 0.0).astype(BF16)
    row_params = nt_dot(by_row_params, params)
    source, target = iota((LANES, LANES), 0), iota((LANES, LANES), 1)
    by_lane_params = jnp.where((source == target + PARAM_LANE) & (target < ALL_HEADS), 1.0, 0.0).astype(BF16)
    skips = jnp.dot(params, by_lane_params, preferred_element_type=F32)
    skip = skips[6:7, :] + skips[7:8, :] + skips[8:9, :]

    def row_param(kind):
        return sum(row_params[:, 3 * kind + part : 3 * kind + part + 1] for part in range(3))

    logits = nt_dot(by_row, notes)
    steps = jnp.log(1.0 + jnp.exp(logits + row_param(1))) * logits[MASK_LANE : MASK_LANE + 1, :]
    token = token_at(iota((span, span), 0), rows, me)
    source = token_at(iota((span, span), 1), rows, me)
    upto = jnp.where(source <= token, 1.0, 0.0)
    sums = nt_dot(-jnp.exp(row_param(0)) * steps, upto, HIGHEST)
    by_token = jnp.concatenate([sums] * (LANES // 32), axis=0).T
    return sums - jnp.log(steps), by_token, skip


def remote_kernel(
    told0, told1, ahead2, ahead3, x0_ref, x1_ref, prior1_ref,
    y_ref, shift_ref, total_ref, skip_ref,
):
    me = lax.axis_index("head")
    rows, width = told0.shape[0], y_ref.shape[1]
    near, head_count = 2 * rows, width // HD
    shift, total, skip = head_sums((told0, told1, ahead2, ahead3), me)
    shift_ref[...] = shift
    total_ref[...] = total
    skip_ref[...] = jnp.broadcast_to(skip, skip_ref.shape)
    block = me ^ 1
    block_shift = rolled(shift, block * head_count, 0)
    block_total = rolled(total[near:], block * head_count, 1)
    mask = jnp.concatenate([ref[:, STATE + MASK_LANE : STATE + MASK_LANE + 1] for ref in (ahead2, ahead3)], axis=0)
    mask = mask.astype(F32)
    out_map = jnp.concatenate([ahead2[:, :STATE], ahead3[:, :STATE]], axis=0)
    from_prior = nt_dot(out_map, prior1_ref[0].reshape(width, STATE))

    def write(from_x):
        for head in range(head_count):
            cols = slice(head * HD, (head + 1) * HD)
            sums = block_total[:, head : head + 1]
            y = from_prior[:, cols] * jnp.exp(sums)
            if from_x is not None:
                y = y + from_x(cols, sums - block_shift[head : head + 1, :near])
            y_ref[:, cols] = (y * mask).astype(BF16)

    @pl.when(me < 2)
    def _():
        in_map = jnp.concatenate([told0[:, IN_MAP], told1[:, IN_MAP]], axis=0)
        products = nt_dot(out_map, in_map)
        x = jnp.concatenate([columns(x0_ref, block, width), columns(x1_ref, block, width)], axis=0)

        def from_x(cols, gaps):
            return jnp.dot((jnp.exp(gaps) * products).astype(BF16), x[:, cols], preferred_element_type=F32)

        write(from_x)

    @pl.when(me >= 2)
    def _():
        write(None)


def near_kernel(
    shift_ref, total_ref, skip_ref, told0, told1, x0_ref, x1_ref, far_ref, relayed_ref,
    prior0_ref, prior1_ref, y_ref,
):
    me = lax.axis_index("head")
    rows, width = told0.shape[0], x0_ref.shape[1] // 4
    near, span, head_count = 2 * rows, 4 * rows, width // HD
    far_map = slice(2 * width, 2 * width + STATE)
    out_map = told0[:, :STATE]
    mask = told0[:, STATE + MASK_LANE : STATE + MASK_LANE + 1].astype(F32)
    shift, total, skip = shift_ref[...], total_ref[:rows, :], skip_ref[...]

    def write(with_far):
        whole = span if with_far else near
        in_map = [told0[:, IN_MAP], told1[:, IN_MAP]]
        if with_far:
            in_map += [far_ref[:, far_map], relayed_ref[:, far_map]]
        products = nt_dot(out_map, jnp.concatenate(in_map, axis=0))
        token = token_at(iota((rows, whole), 0), rows, me)
        source = token_at(iota((rows, whole), 1), rows, me)
        causal = jnp.where(source <= token, 0.0, -jnp.inf)
        for hop in range(4):
            block = me ^ hop
            block_shift = rolled(shift, block * head_count, 0)
            block_total = rolled(total, block * head_count, 1)
            block_skip = rolled(skip, block * head_count, 1)[0:1, :]
            own = columns(x0_ref, block, width)
            sources = [own, columns(x1_ref, block, width)]
            reach = near
            if hop < 2:
                reach = whole
                from_prior = nt_dot(out_map, (prior0_ref, prior1_ref)[hop][0].reshape(width, STATE))
            if reach == span:
                place = (hop, 1 - hop)
                sources += [ref[:, at * width : (at + 1) * width] for ref, at in zip((far_ref, relayed_ref), place)]
            sources = jnp.concatenate(sources, axis=0)
            for head in range(head_count):
                cols = slice(head * HD, (head + 1) * HD)
                sums = block_total[:, head : head + 1]
                weights = jnp.exp(sums - block_shift[head : head + 1, :reach] + causal[:, :reach]) * products[:, :reach]
                y = jnp.dot(weights.astype(BF16), sources[:, cols], preferred_element_type=F32)
                y = y + block_skip[:, head : head + 1] * own[:, cols].astype(F32)
                if hop < 2:
                    y = y + from_prior[:, cols] * jnp.exp(sums)
                y_ref[:, hop * width + head * HD : hop * width + (head + 1) * HD] = y * mask

    @pl.when(me < 2)
    def _():
        write(False)

    @pl.when(me >= 2)
    def _():
        write(True)


def attention_kernel(
    page_map_ref, length_ref, query_ref, pages0, pages1,
    kv0, kv1, far_ref, relayed_ref, told0, told1, told2, told3, out_ref,
):
    me = lax.axis_index("head")
    request = lax.axis_index("dp")
    rows = query_ref.shape[0]
    slots, half = pages0.shape[0], pages0.shape[2]
    part = slots * half
    cached = 2 * part
    inv_scale = 1.0 / math.sqrt(HD)
    square, wide = (slots, slots), (slots, cached)
    holders = jnp.where(iota(square, 0) == iota(square, 1), jnp.broadcast_to(page_map_ref[...], square), 0)
    holders = jnp.sum(holders.astype(F32), axis=1, keepdims=True).astype(jnp.int32)
    page = jnp.where((holders ^ request) == iota(wide, 1) % part // half, iota(wide, 0), 0)
    page = jnp.sum(page.astype(F32), axis=0, keepdims=True).astype(jnp.int32)
    lane = iota((1, cached), 1)
    position = page * PAGE + ((me ^ (lane // part)) % 2) * half + lane % half
    old_shut = jnp.broadcast_to(jnp.where(position < length_ref[...], 0.0, -jnp.inf), (rows, cached))
    ones = jnp.where(iota((8, LANES), 1) == MASK_LANE, 1.0, 0.0).astype(BF16)
    token, source = iota((rows, rows), 0), iota((rows, rows), 1)
    keep = told0[:, STATE + MASK_LANE : STATE + MASK_LANE + 1].astype(F32)
    pages = [ref[:, chip].reshape(part, 2 * HD) for chip in range(2) for ref in (pages0, pages1)]

    def write(reach):
        shut = [old_shut]
        for hop, ref in enumerate((told0, told1, told2, told3)[:reach]):
            real = nt_dot(ones, ref[:, NOTES])[0:1, :] > 0.5
            limit = token if hop == 0 else jnp.where((me ^ hop) < me, rows, -1)
            shut.append(jnp.where(real & (source <= limit), 0.0, -jnp.inf))
        shut = jnp.concatenate(shut, axis=1)
        shut = jnp.concatenate([shut] * GROUP, axis=0)
        for group in range(KVH):
            queries = jnp.concatenate(
                [query_ref[:, (group * GROUP + h) * HD : (group * GROUP + h + 1) * HD] for h in range(GROUP)],
                axis=0,
            )
            here = jnp.broadcast_to(me // 2, (part, 2 * HD)) == group
            every = [jnp.where(here, pages[core], pages[core ^ 2]) for core in range(2)]
            for ref in (kv0, kv1, far_ref, relayed_ref)[:reach]:
                start = ref.shape[1] - KEYVALS + 2 * group * HD
                every.append(ref[:, start : start + 2 * HD])
            every = jnp.concatenate(every, axis=0)
            keys, values = every[:, :HD], every[:, HD:]
            scores = nt_dot(queries, keys) * inv_scale + shut
            top = jnp.max(scores, axis=1, keepdims=True)
            terms = jnp.exp(scores - top)
            total = jnp.sum(terms, axis=1, keepdims=True)
            mixed = jnp.dot(terms.astype(BF16), values, preferred_element_type=F32) / total
            for h in range(GROUP):
                head = group * GROUP + h
                out_ref[:, head * HD : (head + 1) * HD] = (mixed[h * rows : (h + 1) * rows] * keep).astype(BF16)

    @pl.when(me < 2)
    def _():
        write(2)

    @pl.when(me >= 2)
    def _():
        write(4)


def final_kernel(attended_ref, gate_ref, gain_ref, y_ref, y2_ref, y3_ref, out_ref, gated, normed, sems):
    me = lax.axis_index("head")
    rows, width = y_ref.shape[0], y2_ref.shape[1]
    heads_width = attended_ref.shape[1]
    first = pltpu.make_async_copy(attended_ref, out_ref.at[:, pl.ds(0, heads_width)], sems.at[4])
    first.start()
    squares = jnp.zeros((rows, 1), F32)
    for hop, far in enumerate((None, None, y3_ref[rows:, :], y2_ref[:rows, :])):
        gate = columns(gate_ref, me ^ hop, width).astype(F32)
        part = y_ref[:, hop * width : (hop + 1) * width]
        if far is not None:
            part = part + far.astype(F32)
        part = part.astype(BF16).astype(F32) * (gate / (1.0 + jnp.exp(-gate)))
        gated[:, hop * width : (hop + 1) * width] = part
        squares = squares + jnp.sum(part * part, axis=1, keepdims=True)
    scale = lax.rsqrt(squares / MI + EPSILON)
    copies = [first]
    for hop in range(4):
        gain = columns(gain_ref, me ^ hop, width)
        normed[hop] = (gated[:, hop * width : (hop + 1) * width] * scale * gain).astype(BF16)
        start = pl.multiple_of(heads_width + (me ^ hop) * width, LANES)
        copy = pltpu.make_async_copy(normed.at[hop], out_ref.at[:, pl.ds(start, width)], sems.at[hop])
        copy.start()
        copies.append(copy)
    for copy in copies:
        copy.wait()


def behind(block, earlier):
    return lax.optimization_barrier((block, earlier))[0]


def hopped(block, hop):
    return lax.ppermute(block, "head", [(i, i ^ hop) for i in range(4)])


def local(
    queries,
    fresh_keyvals,
    ssm_input,
    gate_input,
    state_maps,
    step_logit,
    slot_mask,
    cache_pool,
    page_map,
    cached_lengths,
    prior_state,
    decay_log,
    step_bias,
    skip_gain,
    norm_gain,
):
    rows = ssm_input.shape[0]
    width = MI // 4
    slots, half = cache_pool.shape[0], cache_pool.shape[1]
    far_pool = hopped(cache_pool, 2)
    pages, sent = call(order_kernel, [((slots // 2, 2, half, 2 * HD), BF16)] * 2, [VMEM] * 2, flops=ORDER_COST)(cache_pool, far_pool)
    told, ahead, far = call(
        pack_kernel,
        [((rows, TOLD), BF16), ((rows, AHEAD), BF16), ((rows, 2 * width + STATE + KEYVALS), BF16)],
        [SMEM] * 3 + [VMEM] * 5,
        limit=60,
        flops=PACK_COST,
    )(
        decay_log, step_bias, skip_gain,
        ssm_input, state_maps, step_logit.T, slot_mask.reshape(1, rows), fresh_keyvals,
    )
    prior1 = hopped(prior_state, 1)
    x1 = hopped(ssm_input, 1)
    kv1 = hopped(fresh_keyvals, 1)
    told1 = hopped(told, 1)
    ahead2 = hopped(ahead, 2)
    far = hopped(far, 2)
    ahead3 = hopped(ahead2, 1)

    parts, bit = [pages], 1
    while bit < slots:
        if bit > 1:
            keep = parts[0].shape[0] // 2
            sent = jnp.concatenate([part[keep:] for part in parts])
            parts = [part[:keep] for part in parts]
        if bit == 2:
            sent = behind(sent, told1)
        came = lax.ppermute(sent, "dp", [(i, i ^ bit) for i in range(slots)])
        keep = parts[0].shape[0]
        parts = parts + [came[i * keep : (i + 1) * keep] for i in range(len(parts))]
        bit *= 2
    y2, shift, total, skip = call(
        remote_kernel,
        [((2 * rows, width), BF16), ((32, 4 * rows), F32), ((4 * rows, LANES), F32), ((8, LANES), F32)],
        [VMEM] * 7,
        flops=SCAN_COST,
    )(told, told1, ahead2, ahead3, ssm_input, x1, prior1)
    relayed = hopped(behind(far, y2), 1)
    y2 = hopped(y2, 2)
    (y,) = call(near_kernel, [((rows, MI), F32)], [VMEM] * 11)(
        shift, total, skip, told, told1, ssm_input, x1, far, relayed, prior_state, prior1
    )
    y3 = hopped(behind(y2, y), 1)
    pages = jnp.concatenate(parts)
    pages1 = hopped(pages, 1)
    (attended,) = call(attention_kernel, [((rows, QH * HD), BF16)], [VMEM] * 13, flops=ATTEND_COST)(
        page_map, cached_lengths.reshape(1, 1), queries, pages, pages1,
        fresh_keyvals, kv1, far, relayed, told, told1, ahead2, ahead3,
    )
    (result,) = call(
        final_kernel,
        [((rows, QH * HD + MI), BF16)],
        [VMEM] * 6,
        [
            pltpu.VMEM((rows, MI), F32),
            pltpu.VMEM((4, rows, width), BF16),
            pltpu.SemaphoreType.DMA((5,)),
        ],
        out_spec=ANY,
    )(attended, gate_input, norm_gain.reshape(1, MI), y, y2, y3)
    return result


def solution(mesh):
    in_specs = (
        P(("dp", "head"), None),
        P(("dp", "head"), None),
        P(("dp", "head"), None),
        P(("dp", "head"), None),
        P(("dp", "head"), None),
        P(("dp", "head"), None),
        P(("dp", "head")),
        P("dp", "head", None),
        P("dp", None),
        P("dp"),
        P("dp", "head", None, None),
        P("head"),
        P("head"),
        P("head"),
        P(),
    )
    out_specs = P(("dp", "head"), None)
    return jax.shard_map(local, mesh=mesh, in_specs=in_specs, out_specs=out_specs, check_vma=False)
```
